128 devices in a mesh: section: 2 (over core), expert: 16 (over z, y), head: 4 (over x).
Axes of the slice: x: 4, y: 4, z: 4, core: 2. Of those that a mesh axis runs over, the one named last changes fastest.
Arguments:
- inputs: bfloat16 [2, 2048, 768], P(None, 'expert'), may hold values from -6 to 6
- cotangent: bfloat16 [2, 2048, 768], P(None, 'expert'), may hold values from -6 to 6
- routes: int32 [2, 2, 2048, 2], P('section', None, 'expert'), may hold values from 0 to 31, all different within a row; in each aligned block of 128 rows (0 to 127, 128 to 255, ..., all dimensions but the last counted through in order) at most 12 rows name the same one
- attend_gain: bfloat16 [2, 768], P('section'), may hold values from 0.099609375 to 1.8984375
- query_key_value: bfloat16 [2, 3, 768, 768], P('section', None, None, 'head'), may hold values from -0.21875 to 0.21875
- attend_out: bfloat16 [2, 768, 768], P('section', 'head'), may hold values from -1.75 to 1.75
- position_bias: bfloat16 [2, 12, 32], P('section', 'head'), may hold values from -4 to 4
- mixture_gain: bfloat16 [2, 768], P('section'), may hold values from 0.099609375 to 1.8984375
- router: bfloat16 [2, 768, 32], P('section'), may hold values from -0.15625 to 0.15625
- expert_up: bfloat16 [2, 32, 768, 3072], P('section', 'expert', None, 'head'), may hold values from -0.21875 to 0.21875
- expert_down: bfloat16 [2, 32, 3072, 768], P('section', 'expert', 'head'), may hold values from -0.109375 to 0.109375
Outputs:
- section_output: bfloat16 [2, 2, 2048, 768], P('section', None, 'expert')
- input_grad: float32 [2, 2, 2048, 768], P('section', None, 'expert')
- grad_attend_gain: float32 [2, 768], P('section')
- grad_query_key_value: float32 [2, 3, 768, 768], P('section', None, None, 'head')
- grad_attend_out: float32 [2, 768, 768], P('section', 'head')
- grad_position_bias: float32 [2, 12, 32], P('section', 'head')
- grad_mixture_gain: float32 [2, 768], P('section')
- grad_router: float32 [2, 768, 32], P('section')
- grad_expert_up: float32 [2, 32, 768, 3072], P('section', 'expert', None, 'head')
- grad_expert_down: float32 [2, 32, 3072, 768], P('section', 'expert', 'head')
The draws below stay inside these ranges and needn't reach their ends.
Inputs may be any that keep to these rules, and one draw needn't show every extreme that they name: `routes`: each token names two different experts. Among the 128 tokens of one sequence (one section, micro-batch and index of expert), no expert is named more than 12 times over both slots, and in every draw some expert is named exactly 12 times by some sequence.
All inputs are finite; a program needn't handle non-finite values.
Results may differ from the reference program's by a relative error of at most 0.028.
Values may be sent and summed in bfloat16 or wider, within the bound.
No kernel may reach another device: no remote copies, remote signals or barrier semaphores. Data moves between devices by JAX's collectives and lax.ppermute only.
A program may use at most 128 MiB of HBM per device.

```python
import math
import jax
import jax.numpy as jnp
import numpy as np
from jax import lax

D = 768
HEADS = 12
HEAD_DIM = 64
FF = 3072
NB = 32
SEQ = 128
MICRO = 2
EXPERTS = 32
CAP = 12
TOKENS = 2048
N_EXPERT = 16


def shard_levels(own_key, extent, shards, least, top_value):
    def one(axis_at, blocks):
        draws = jax.random.uniform(jax.random.fold_in(jax.random.fold_in(own_key, 6), axis_at), (blocks,), jnp.float32, least / len(shards), top_value / len(shards))
        return jnp.repeat(jnp.exp(draws), extent[axis_at] // blocks).reshape((-1,) + (1,) * (len(extent) - axis_at - 1))

    level = one(*shards[0])
    for cut in shards[1:]:
        level = level * one(*cut)
    return level


def assign_block(key, own, number, rows, number_of, top, most, skew):
    ranking = jax.random.permutation(key, number_of)
    heavy_load, common = load_shares(number_of, rows * top, most, skew, True), load_shares(number_of, rows * top, most, skew, False)
    places = jnp.arange(number_of)

    def named(lengths, turn):
        used = int((lengths > 0).sum())
        fixed = max(1, used // 4)
        moved = fixed + (places - fixed + turn * (used - fixed)) % max(1, number_of - fixed)
        return jnp.zeros((number_of,), jnp.int32).at[ranking[jnp.where(places < fixed, places, moved)]].set(jnp.asarray(lengths, jnp.int32))

    lengths = jnp.where(number % 4 == 0, named(heavy_load, number // 4), named(common, number - number // 4 - 1))
    mixed = jax.random.permutation(jax.random.fold_in(own, 3), number_of)
    giver, taker = mixed[0:number_of // 2 * 2:2], mixed[1:number_of // 2 * 2:2]
    slack = jnp.minimum(lengths[giver] - 1, most - lengths[taker]) // 2
    slack = jnp.where((giver == ranking[0]) | (taker == ranking[0]) | (lengths[taker] == 0), 0, jnp.maximum(slack, 0))
    moved = jax.random.randint(jax.random.fold_in(own, 4), (number_of // 2,), 0, 1 << 20) % (slack + 1)
    lengths = lengths.at[giver].add(-moved).at[taker].add(moved)
    items = jnp.searchsorted(jnp.cumsum(lengths), jnp.arange(rows * top), side="right").astype(jnp.int32)
    table = items.reshape(top, rows).T
    table = table[jax.random.permutation(jax.random.fold_in(own, 1), rows)]
    turn = jax.random.randint(jax.random.fold_in(own, 2), (rows, 1), 0, top)
    return jnp.take_along_axis(table, (jnp.arange(top)[None, :] + turn) % top, axis=1)


def load_shares(count, total, most, lean, full):
    weights = [(1 << 20) // math.isqrt(standing ** lean) + 1 for standing in range(1, count + 1)]
    largest = most if full else min(most, max(-(-total // count), total * weights[0] // sum(weights)))
    least = 1 if total - largest >= count - 1 else 0
    holding, surplus = [largest] + [least] * (count - 1), total - largest - least * (count - 1)
    while surplus > 0:
        free = [i for i in range(1, count) if holding[i] < largest] or [i for i in range(1, count) if holding[i] < most]
        pool, remaining = sum([weights[i] for i in free]), surplus
        for i in free:
            more = min(most - holding[i], max(1, remaining * weights[i] // pool), surplus)
            holding[i] = holding[i] + more
            surplus = surplus - more
    return np.array(holding)


def gaussian(stream_key, shape, scale, bound, cuts=(), held_as=jnp.bfloat16):
    entries = scale * jax.random.normal(stream_key, shape, jnp.float32)
    if cuts:
        entries = entries * shard_levels(stream_key, shape, cuts, -0.22, 0.18)
    return jnp.clip(entries, -bound, bound).astype(held_as)


def setup_inputs(seed: int = 0) -> dict:
    key_list = jax.random.split(jax.random.key(seed), 12)
    inputs = gaussian(key_list[0], (MICRO, TOKENS, D), 1.0, 6.0, ((1, 16),))
    cotangent = gaussian(key_list[1], (MICRO, TOKENS, D), 1.0, 6.0, ((1, 16),))
    routes_keys = jax.random.split(jax.random.fold_in(key_list[2], 1), 2 * MICRO * TOKENS // SEQ)
    routes_turns = jax.random.permutation(jax.random.fold_in(key_list[2], 3), 2 * MICRO * TOKENS // SEQ)
    routes = jax.vmap(lambda own, number: assign_block(jax.random.fold_in(key_list[2], 2), own, number, SEQ, EXPERTS, 2, CAP, 2))(routes_keys, routes_turns).reshape((2, MICRO, TOKENS, 2))
    attend_gain = jnp.clip(1.0 + 0.18 * jax.random.normal(key_list[3], (2, D), jnp.float32), 0.099609375, 1.8984375).astype(jnp.bfloat16)
    query_key_value = gaussian(key_list[4], (2, 3, D, D), D ** -0.5, 0.21875, ((0, 2), (3, 4)))
    attend_out = gaussian(key_list[5], (2, D, D), (2 * D // SEQ) ** -0.5, 1.75, ((0, 2), (1, 4)))
    position_bias = gaussian(key_list[6], (2, HEADS, NB), 1.0, 4.0, ((0, 2), (1, 4)))
    mixture_gain = jnp.clip(1.0 + 0.18 * jax.random.normal(key_list[7], (2, D), jnp.float32), 0.099609375, 1.8984375).astype(jnp.bfloat16)
    router = gaussian(key_list[8], (2, D, EXPERTS), (2 * D) ** -0.5, 0.15625, ((0, 2),))
    expert_up = gaussian(key_list[9], (2, EXPERTS, D, FF), D ** -0.5, 0.21875, ((0, 2), (1, 16), (3, 4)))
    expert_down = gaussian(key_list[10], (2, EXPERTS, FF, D), FF ** -0.5, 0.109375, ((0, 2), (1, 16), (2, 4)))
    return dict(inputs=inputs, cotangent=cotangent, routes=routes, attend_gain=attend_gain, query_key_value=query_key_value, attend_out=attend_out, position_bias=position_bias, mixture_gain=mixture_gain, router=router, expert_up=expert_up, expert_down=expert_down)


EPS = 1e-06
NEG = -1e+30
HIGH = lax.Precision.HIGHEST

@jax.custom_vjp
def low(v):
    return lax.optimization_barrier(v.astype(jnp.bfloat16)).astype(jnp.float32)

@jax.custom_vjp
def low_back(v):
    return v

def low_keep(v):
    return (low(v), None)

def low_pass(kept, grad):
    return (grad,)

def back_keep(v):
    return (v, None)

def back_low(kept, grad):
    return (low(grad),)
low.defvjp(low_keep, low_pass)
low_back.defvjp(back_keep, back_low)

def rms_norm(values, gain):
    return values * lax.rsqrt(lax.optimization_barrier(jnp.mean(values * values, axis=-1, keepdims=True)) + EPS) * gain

def slot_targets(route_tile, experts, capacity):
    flat = route_tile.reshape(-1).astype(jnp.int32)
    levels = lax.broadcasted_iota(jnp.int32, (flat.shape[0], experts), 1)
    onehot = (flat[:, None] == levels).astype(jnp.int32)
    place = lax.optimization_barrier(jnp.sum((jnp.cumsum(onehot, axis=0) - 1) * onehot, axis=1))
    return (flat * capacity + place).astype(jnp.int32)

def attend(normed, proj_weight, out_weight, table):
    length = normed.shape[0]
    projected = low_back(low(jnp.einsum('sd,kde->kse', normed, proj_weight, precision=HIGH)))
    heads = projected.reshape(3, length, HEADS, HEAD_DIM)
    rows = lax.broadcasted_iota(jnp.int32, (length, length), 0)
    cols = lax.broadcasted_iota(jnp.int32, (length, length), 1)
    offset = rows - cols
    bias = table[:, jnp.clip(offset, 0, NB - 1)]
    scores = jnp.einsum('shd,thd->hst', heads[0], heads[1], precision=HIGH) * HEAD_DIM ** (-0.5) + bias
    scores = low_back(scores)
    masked = jnp.where(offset[None] >= 0, scores, NEG)
    top = lax.optimization_barrier(jnp.max(masked, axis=-1, keepdims=True))
    weights = jnp.exp(masked - top)
    probs = weights / lax.optimization_barrier(jnp.sum(weights, axis=-1, keepdims=True))
    mixed = jnp.einsum('hst,thd->shd', low(probs), heads[2], precision=HIGH)
    mixed = low_back(low(mixed.reshape(length, HEADS * HEAD_DIM)))
    return low_back(jnp.dot(mixed, out_weight, precision=HIGH, preferred_element_type=jnp.float32))

def expert_apply(rows, up_weight, down_weight):
    pre_act = low_back(jnp.dot(rows, up_weight, precision=HIGH, preferred_element_type=jnp.float32))
    hidden = low(jax.nn.gelu(pre_act))
    return jnp.dot(hidden, down_weight, precision=HIGH, preferred_element_type=jnp.float32)

def mixture(normed, route_tile, router_weight, up_weight, down_weight):
    blocks = normed.shape[0]
    width = normed.shape[-1]
    capacity = 3 * SEQ // EXPERTS
    target = jax.vmap(lambda tile: slot_targets(tile, EXPERTS, capacity))(route_tile)
    rows = jnp.repeat(normed, 2, axis=1)

    def place(where_to, values):
        return jnp.zeros((EXPERTS * capacity, width), normed.dtype).at[where_to].set(values)
    buffer = jax.vmap(place)(target, rows)
    buffer = buffer.reshape(blocks, EXPERTS, capacity, width).transpose(1, 0, 2, 3)
    buffer = buffer.reshape(EXPERTS, blocks * capacity, width)
    results = lax.map(jax.checkpoint(lambda item: expert_apply(item[0], item[1], item[2])), (buffer, up_weight, down_weight))
    results = results.reshape(EXPERTS, blocks, capacity, width).transpose(1, 0, 2, 3)
    results = results.reshape(blocks, EXPERTS * capacity, width)
    slots = jax.vmap(lambda table, where_from: table[where_from])(results, target)
    slots = low_back(slots.reshape(blocks, SEQ, 2, width))
    logits = low_back(jnp.einsum('bsd,de->bse', normed, router_weight, precision=HIGH))
    levels = lax.broadcasted_iota(jnp.int32, route_tile.shape + (EXPERTS,), 3)
    pick = (route_tile[..., None] == levels).astype(normed.dtype)
    chosen = lax.optimization_barrier(jnp.sum(logits[:, :, None, :] * pick, axis=-1))
    top = lax.optimization_barrier(jnp.max(chosen, axis=-1, keepdims=True))
    weights = jnp.exp(chosen - top)
    gates = weights / lax.optimization_barrier(jnp.sum(weights, axis=-1, keepdims=True))
    return lax.optimization_barrier(jnp.sum(gates[..., None] * slots, axis=2))

def layer(values, gain_a, proj_weight, out_weight, table, gain_m, router_weight, up_weight, down_weight, route_tile):
    normed_a = low(rms_norm(values, gain_a))
    sequences = normed_a.reshape(MICRO * N_EXPERT, SEQ, D)
    attended = lax.map(jax.checkpoint(lambda one: attend(one, proj_weight, out_weight, table)), sequences)
    middle = values + attended.reshape(values.shape)
    normed_m = low(rms_norm(middle, gain_m))
    mixed = mixture(normed_m.reshape(MICRO * N_EXPERT, SEQ, D), route_tile.reshape(MICRO * N_EXPERT, SEQ, 2), router_weight, up_weight, down_weight)
    return middle + mixed.reshape(values.shape)

def reference(inputs, cotangent, routes, attend_gain, query_key_value, attend_out, position_bias, mixture_gain, router, expert_up, expert_down):
    params = (attend_gain.astype(jnp.float32), query_key_value.astype(jnp.float32), attend_out.astype(jnp.float32), position_bias.astype(jnp.float32), mixture_gain.astype(jnp.float32), router.astype(jnp.float32), expert_up.astype(jnp.float32), expert_down.astype(jnp.float32))
    start = inputs.astype(jnp.float32)
    probe = jnp.zeros_like(start)

    def forward(values, extra, gain_a, proj_weight, out_weight, table, gain_m, router_weight, up_weight, down_weight):
        first = layer(values, gain_a[0], proj_weight[0], out_weight[0], table[0], gain_m[0], router_weight[0], up_weight[0], down_weight[0], routes[0])
        sent = low_back(low(first)) + extra
        second = layer(sent, gain_a[1], proj_weight[1], out_weight[1], table[1], gain_m[1], router_weight[1], up_weight[1], down_weight[1], routes[1])
        return (second, first)
    second, back_fn, first = jax.vjp(forward, start, probe, *params, has_aux=True)
    grads = back_fn(cotangent.astype(jnp.float32))
    section_output = jnp.stack([first, second]).astype(jnp.bfloat16)
    input_grad = jnp.stack([grads[0], grads[1]])
    return (section_output, input_grad, grads[2], grads[3], grads[4], grads[5], grads[6], grads[7], grads[8], grads[9])
```

```python
import jax
import jax.numpy as jnp
from jax import lax
from jax.sharding import PartitionSpec as P

HEAD_DIM = 64
EPS = 1e-06
NEG = -1e30
F32 = jnp.float32
BF16 = jnp.bfloat16


def swap(array):
    return lax.ppermute(array, "section", [(0, 1), (1, 0)])


def ring(array, axis, by):
    size = lax.axis_size(axis)
    return lax.ppermute(array, axis, [(i, (i + by) % size) for i in range(size)])


def head_sum(part):
    far = ring(part, "head", 2)
    left = ring(part, "head", 1)
    right = ring(part, "head", -1)
    return (part.astype(F32) + far.astype(F32)) + (left.astype(F32) + right.astype(F32))


def exchange(rows):
    size = lax.axis_size("expert")
    blocks = rows.reshape(size, rows.shape[0] // size, rows.shape[1])
    return lax.all_to_all(blocks, "expert", 0, 0, tiled=True)


def mm(a, b, dims):
    return lax.dot_general(a, b, (dims, ((), ())), preferred_element_type=F32)


def norm_scale(values):
    return lax.rsqrt(jnp.mean(values * values, axis=-1, keepdims=True) + EPS)


def norm_back(grad_normed, values, scale, gain):
    unit = values * scale
    grad_gain = jnp.sum(grad_normed * unit, axis=0)
    grad_unit = grad_normed * gain
    grad_values = scale * (grad_unit - unit * jnp.mean(grad_unit * unit, axis=-1, keepdims=True))
    return (grad_values, grad_gain)


def position_tables(length, buckets):
    rows = lax.broadcasted_iota(jnp.int32, (length, length), 0)
    cols = lax.broadcasted_iota(jnp.int32, (length, length), 1)
    offset = rows - cols
    levels = lax.broadcasted_iota(jnp.int32, (buckets, length, length), 0)
    onehot = (jnp.clip(offset, 0, buckets - 1)[None] == levels).astype(BF16)
    return (offset >= 0, onehot)


def attend_scores(heads, table, causal, onehot):
    bias = jnp.einsum("bst,hb->hst", onehot, table, preferred_element_type=F32)
    scores = jnp.einsum("shd,thd->hst", heads[0], heads[1], preferred_element_type=F32)
    scores = scores * HEAD_DIM ** (-0.5) + bias
    return jnp.where(causal[None], scores, NEG)


def attend_forward(normed, proj_weight, out_weight, table, causal, onehot):
    length = normed.shape[0]
    local_heads = table.shape[0]
    projected = jnp.einsum("sd,kde->kse", normed, proj_weight, preferred_element_type=F32)
    projected = projected.astype(BF16)
    heads = projected.reshape(3, length, local_heads, HEAD_DIM)
    scores = attend_scores(heads, table, causal, onehot)
    top = jnp.max(scores, axis=-1, keepdims=True)
    weights = jnp.exp(scores - top)
    probs = weights / jnp.sum(weights, axis=-1, keepdims=True)
    mixed = jnp.einsum("hst,thd->shd", probs.astype(BF16), heads[2], preferred_element_type=F32)
    mixed = mixed.reshape(length, local_heads * HEAD_DIM).astype(BF16)
    return (mm(mixed, out_weight, ((1,), (0,))), (projected, mixed, probs))


def attend_backward(grad_attn, proj_weight, out_weight, onehot, saved_attn):
    projected, mixed, probs = saved_attn
    length = projected.shape[1]
    local_heads = probs.shape[0]
    heads = projected.reshape(3, length, local_heads, HEAD_DIM)
    grad_mixed = mm(grad_attn, out_weight, ((1,), (1,)))
    grad_mixed = grad_mixed.astype(BF16).reshape(length, local_heads, HEAD_DIM)
    grad_probs = jnp.einsum("shd,thd->hst", grad_mixed, heads[2], preferred_element_type=F32)
    delta = jnp.sum(probs * grad_probs, axis=-1, keepdims=True)
    grad_scores = (probs * (grad_probs - delta)).astype(BF16)
    grad_table = jnp.einsum("bst,hst->hb", onehot, grad_scores, preferred_element_type=F32)
    factor = HEAD_DIM ** (-0.5)
    grad_query = factor * jnp.einsum("hst,thd->shd", grad_scores, heads[1], preferred_element_type=F32)
    grad_key = factor * jnp.einsum("hst,shd->thd", grad_scores, heads[0], preferred_element_type=F32)
    grad_value = jnp.einsum("hst,shd->thd", probs.astype(BF16), grad_mixed, preferred_element_type=F32)
    grad_projected = (
        jnp.stack([grad_query, grad_key, grad_value])
        .reshape(3, length, local_heads * HEAD_DIM)
        .astype(BF16)
    )
    grad_normed = jnp.einsum("kse,kde->sd", grad_projected, proj_weight, preferred_element_type=F32)
    return (grad_normed, grad_projected, grad_table)


def slot_masks(route_tile, experts, capacity):
    length = route_tile.shape[0]
    levels = lax.broadcasted_iota(jnp.int32, (length, 2, experts), 2)
    pick = (route_tile[:, :, None] == levels).astype(F32)
    named = jnp.sum(pick, axis=1).astype(BF16)
    rows = lax.broadcasted_iota(jnp.int32, (length, length), 0)
    cols = lax.broadcasted_iota(jnp.int32, (length, length), 1)
    before = mm((cols < rows).astype(BF16), named, ((1,), (0,)))
    place = jnp.sum(before[:, None, :] * pick, axis=-1).astype(jnp.int32)
    target = route_tile * capacity + place
    slots = lax.broadcasted_iota(jnp.int32, (length, experts * capacity), 1)
    masks = [(target[:, k : k + 1] == slots) for k in range(2)]
    return (pick, masks)


def by_expert(blocks, local_experts):
    size, rows, width = blocks.shape
    blocks = blocks.reshape(size, local_experts, rows // local_experts, width)
    return blocks.transpose(1, 0, 2, 3).reshape(local_experts, -1, width)


def by_source(rows, sources):
    local_experts, count, width = rows.shape
    rows = rows.reshape(local_experts, sources, count // sources, width)
    return rows.transpose(1, 0, 2, 3).reshape(-1, width)


def layer_forward(values, routing, params, tables):
    gain_a, proj_weight, out_weight, table, gain_m, router_t, up_weight, down_weight = params
    pick, masks = routing
    scale_a = norm_scale(values)
    normed_a = (values * scale_a * gain_a).astype(BF16)
    partial_attn, saved_attn = attend_forward(normed_a, proj_weight, out_weight, table, *tables)
    middle = values + head_sum(partial_attn.astype(BF16))
    scale_m = norm_scale(middle)
    normed_m = (middle * scale_m * gain_m).astype(BF16)
    logits = mm(normed_m, router_t, ((1,), (1,)))
    chosen = jnp.sum(logits[:, None, :] * pick, axis=-1)
    top = jnp.max(chosen, axis=-1, keepdims=True)
    weights = jnp.exp(chosen - top)
    gates = weights / jnp.sum(weights, axis=-1, keepdims=True)
    spread = (masks[0] | masks[1]).astype(BF16)
    buffer = mm(spread, normed_m, ((0,), (0,))).astype(BF16)
    arrived = by_expert(exchange(buffer), up_weight.shape[0])
    pre_act = jnp.einsum("erd,edf->erf", arrived, up_weight, preferred_element_type=F32)
    hidden = jax.nn.gelu(pre_act).astype(BF16)
    rows = jnp.einsum("erf,efd->erd", hidden, down_weight, preferred_element_type=F32).astype(BF16)
    returned = exchange(by_source(rows, lax.axis_size("expert"))).reshape(buffer.shape)
    slots = [mm(mask.astype(BF16), returned, ((1,), (0,))) for mask in masks]
    mixed_rows = gates[:, 0:1] * slots[0] + gates[:, 1:2] * slots[1]
    layer_out = middle + head_sum(mixed_rows.astype(BF16))
    gap = slots[0] - slots[1]
    saved = (values, scale_a, normed_a, saved_attn, middle, scale_m, normed_m, gates, gap, spread)
    return (layer_out, saved, (arrived, pre_act, hidden))


def layer_backward(grad_low, saved, kept, routing, params, tables):
    gain_a, proj_weight, out_weight, table, gain_m, router_t, up_weight, down_weight = params
    values, scale_a, normed_a, saved_attn, middle, scale_m, normed_m, gates, gap, spread = saved
    arrived, pre_act, hidden = kept
    pick, masks = routing
    grad_out = grad_low.astype(F32)
    weighted = jnp.where(masks[0], gates[:, 0:1], jnp.where(masks[1], gates[:, 1:2], 0.0))
    high = weighted.astype(BF16)
    rest = (weighted - high.astype(F32)).astype(BF16)
    grad_buffer = mm(high, grad_low, ((0,), (0,))) + mm(rest, grad_low, ((0,), (0,)))
    grad_arrived = by_expert(exchange(grad_buffer.astype(BF16)), up_weight.shape[0])
    difference = jnp.sum(grad_out * gap, axis=-1, keepdims=True)
    grad_hidden = jnp.einsum("erd,efd->erf", grad_arrived, down_weight, preferred_element_type=F32)
    unused, gelu_back = jax.vjp(jax.nn.gelu, pre_act)
    grad_pre = gelu_back(grad_hidden)[0].astype(BF16)
    grad_rows = jnp.einsum("erf,edf->erd", grad_pre, up_weight, preferred_element_type=F32)
    grad_rows = by_source(grad_rows.astype(BF16), lax.axis_size("expert"))
    returned = exchange(grad_rows).reshape(spread.shape[1], -1)
    part = mm(spread, returned, ((1,), (0,))).astype(BF16)
    head = difference.astype(BF16)
    tail = (difference - head.astype(F32)).astype(BF16)
    side = jnp.concatenate([head, tail, jnp.zeros((part.shape[0], 126), BF16)], axis=1)
    total = head_sum(jnp.concatenate([part, side], axis=1))
    width = values.shape[1]
    grad_normed_m = total[:, :width]
    difference = total[:, width : width + 1] + total[:, width + 1 : width + 2]
    grad_first = gates[:, 0:1] * gates[:, 1:2] * difference
    grad_logits = (grad_first * pick[:, 0] - grad_first * pick[:, 1]).astype(BF16)
    grad_router = mm(grad_logits, normed_m, ((0,), (0,)))
    grad_normed_m = grad_normed_m + mm(grad_logits, router_t, ((1,), (0,)))
    grad_middle, grad_gain_m = norm_back(grad_normed_m, middle, scale_m, gain_m)
    grad_middle = grad_middle + grad_out
    grad_attn = grad_middle.astype(BF16)
    grad_normed_a, grad_projected, grad_table = attend_backward(
        grad_attn, proj_weight, out_weight, tables[1], saved_attn
    )
    grad_normed_a = head_sum(grad_normed_a.astype(BF16))
    grad_values, grad_gain_a = norm_back(grad_normed_a, values, scale_a, gain_a)
    small = jnp.concatenate(
        [
            grad_router,
            grad_gain_a[None],
            grad_gain_m[None],
            jnp.pad(grad_table, ((0, 0), (0, width - grad_table.shape[1]))),
            jnp.zeros((3, width), F32),
        ]
    )
    acts = (hidden, grad_arrived, arrived, grad_pre)
    attn_acts = (normed_a, grad_projected, saved_attn[1], grad_attn)
    return (grad_values + grad_middle, acts, attn_acts, small)


def on_device(
    inputs,
    cotangent,
    routes,
    attend_gain,
    query_key_value,
    attend_out,
    position_bias,
    mixture_gain,
    router,
    expert_up,
    expert_down,
):
    length, width = inputs.shape[1:]
    buckets = position_bias.shape[2]
    experts = router.shape[2]
    capacity = 3 * length // experts
    local_heads = position_bias.shape[1]
    first = lax.axis_index("section") == 0

    def own_or(mine, other):
        return (jnp.where(first, mine, other), jnp.where(first, other, mine))

    route_own = jnp.where(first, routes[0, 0], routes[0, 1])
    route_other = swap(jnp.where(first, routes[0, 1], routes[0, 0]))
    route_pair = own_or(route_own, route_other)
    small = jnp.concatenate(
        [
            router[0].T,
            attend_gain,
            mixture_gain,
            jnp.pad(position_bias[0], ((0, 0), (0, width - buckets))),
            jnp.zeros((3, width), BF16),
        ]
    )
    bulk = (small, query_key_value[0], attend_out[0], expert_up[0], expert_down[0])
    pairs = [own_or(array, swap(array)) for array in bulk]
    params = []
    for which in range(2):
        small, proj_weight, out_weight, up_weight, down_weight = [pair[which] for pair in pairs]
        params.append(
            (
                small[experts].astype(F32),
                proj_weight,
                out_weight,
                small[experts + 2 : experts + 2 + local_heads, :buckets],
                small[experts + 1].astype(F32),
                small[:experts],
                up_weight,
                down_weight,
            )
        )
    tables = position_tables(length, buckets)
    routing = [slot_masks(tile, experts, capacity) for tile in route_pair]

    values = jnp.where(first, inputs[0], inputs[1]).astype(F32)
    out_0, saved_0, kept_0 = layer_forward(values, routing[0], params[0], tables)
    low_0 = out_0.astype(BF16)
    out_1, saved_1, kept_1 = layer_forward(low_0.astype(F32), routing[1], params[1], tables)
    low_1 = out_1.astype(BF16)

    grad_low = jnp.where(first, cotangent[0], cotangent[1])
    grad_1, acts_1, attn_acts_1, small_1 = layer_backward(
        grad_low, saved_1, kept_1, routing[1], params[1], tables
    )
    grad_0, acts_0, attn_acts_0, small_0 = layer_backward(
        grad_1.astype(BF16), saved_0, kept_0, routing[0], params[0], tables
    )

    def gathered(pair_0, pair_1, axis):
        sent_1 = lax.ppermute(pair_1, "section", [(0, 1)])
        sent_0 = lax.ppermute(pair_0, "section", [(1, 0)])
        mine = jnp.where(first, pair_0, pair_1)
        other = jnp.where(first, sent_0, sent_1)
        return jnp.concatenate([mine, other], axis=axis)

    hidden, grad_arrived, arrived, grad_pre = [gathered(a, b, 1) for a, b in zip(acts_0, acts_1)]
    grad_down = jnp.einsum("erf,erd->efd", hidden, grad_arrived, preferred_element_type=F32)
    grad_up = jnp.einsum("erd,erf->edf", arrived, grad_pre, preferred_element_type=F32)

    normed_a = gathered(attn_acts_0[0], attn_acts_1[0], 0)
    grad_projected = gathered(attn_acts_0[1], attn_acts_1[1], 1)
    mixed = gathered(attn_acts_0[2], attn_acts_1[2], 0)
    grad_attn = gathered(attn_acts_0[3], attn_acts_1[3], 0)
    grad_proj = jnp.einsum("kse,sd->ked", grad_projected, normed_a, preferred_element_type=F32)
    grad_out_weight = mm(mixed, grad_attn, ((0,), (0,)))
    mine = jnp.where(first, small_0, small_1)
    mine = mine + swap(jnp.where(first, small_1, small_0))
    depth = grad_proj.shape[1]
    packed = jnp.concatenate([grad_proj.reshape(3 * depth, width), grad_out_weight, mine]).astype(BF16)
    size = lax.axis_size("expert")
    share = -(-packed.shape[0] // (8 * size)) * 8
    packed = jnp.pad(packed, ((0, share * size - packed.shape[0]), (0, 0)))
    parts = lax.all_to_all(packed.reshape(size, share, width), "expert", 0, 0, tiled=True)
    summed = jnp.sum(parts.astype(F32), axis=0).astype(BF16)
    whole = lax.all_to_all(
        jnp.broadcast_to(summed[None], (size, share, width)), "expert", 0, 0, tiled=True
    )
    whole = whole.reshape(share * size, width).astype(F32)
    grad_proj = whole[: 3 * depth].reshape(3, depth, width).transpose(0, 2, 1)
    grad_out_weight = whole[3 * depth : 4 * depth]
    small = whole[4 * depth :]

    section_output = jnp.stack(
        [
            jnp.where(first, low_0, lax.ppermute(low_1, "section", [(0, 1)])),
            jnp.where(first, lax.ppermute(low_0, "section", [(1, 0)]), low_1),
        ]
    )
    input_grad = jnp.stack(
        [
            jnp.where(first, grad_0, lax.ppermute(grad_1, "section", [(0, 1)])),
            jnp.where(first, lax.ppermute(grad_0, "section", [(1, 0)]), grad_1),
        ]
    )
    return (
        section_output[None],
        input_grad[None],
        small[experts][None],
        grad_proj[None],
        grad_out_weight[None],
        small[experts + 2 : experts + 2 + local_heads, :buckets][None],
        small[experts + 1][None],
        small[:experts].T[None],
        grad_up[None],
        grad_down[None],
    )


def solution(mesh):
    return jax.shard_map(
        on_device,
        mesh=mesh,
        in_specs=(
            P(None, "expert", None),
            P(None, "expert", None),
            P("section", None, "expert", None),
            P("section", None),
            P("section", None, None, "head"),
            P("section", "head", None),
            P("section", "head", None),
            P("section", None),
            P("section", None, None),
            P("section", "expert", None, "head"),
            P("section", "expert", "head", None),
        ),
        out_specs=(
            P("section", None, "expert", None),
            P("section", None, "expert", None),
            P("section", None),
            P("section", None, None, "head"),
            P("section", "head", None),
            P("section", "head", None),
            P("section", None),
            P("section", None, None),
            P("section", "expert", None, "head"),
            P("section", "expert", "head", None),
        ),
        check_vma=False,
    )
```

```python
import functools

import jax
import jax.numpy as jnp
import ml_dtypes
import numpy as np
from jax import lax
from jax.experimental import pallas as pl
from jax.experimental.pallas import tpu as pltpu
from jax.sharding import PartitionSpec as P

HEAD_DIM = 64
EPS = 1e-06
NEG = -1e30
F32 = jnp.float32
BF16 = jnp.bfloat16
GAIN_A, GAIN_M, TABLE, SMALL = 32, 40, 48, 64

VMEM = pl.BlockSpec(memory_space=pltpu.VMEM)
SMEM = pl.BlockSpec(memory_space=pltpu.SMEM)
ANY = pl.BlockSpec(memory_space=pl.ANY)


def call(kernel, name, out_shape, in_specs, args, scratch=(), out_specs=None, flops=10**9, size=2**20):
    return pl.pallas_call(
        kernel,
        name=name,
        out_shape=[jax.ShapeDtypeStruct(shape, dtype) for shape, dtype in out_shape],
        in_specs=in_specs,
        out_specs=out_specs or [VMEM] * len(out_shape),
        scratch_shapes=list(scratch),
        compiler_params=pltpu.CompilerParams(vmem_limit_bytes=48 * 2**20),
        cost_estimate=pl.CostEstimate(flops=flops, bytes_accessed=size, transcendentals=0),
    )(*args)


def nn(a, b):
    return lax.dot_general(a, b, (((1,), (0,)), ((), ())), preferred_element_type=F32)


def nt(a, b):
    return lax.dot_general(a, b, (((1,), (1,)), ((), ())), preferred_element_type=F32)


def tn(a, b):
    return lax.dot_general(a, b, (((0,), (0,)), ((), ())), preferred_element_type=F32)


def iota(shape, dim):
    return lax.broadcasted_iota(jnp.int32, shape, dim)


def ones_where(mask):
    return jnp.where(mask, 1.0, 0.0)


def flipped(array):
    return array.astype(F32).T.astype(BF16)


def norm_scale(values):
    return lax.rsqrt(jnp.mean(values * values, axis=-1, keepdims=True) + EPS)


def norm_back(grad_normed, values, scale, gain):
    unit = values * scale
    grad_gain = jnp.sum(grad_normed * unit, axis=0, keepdims=True)
    grad_unit = grad_normed * gain
    grad_values = scale * (grad_unit - unit * jnp.mean(grad_unit * unit, axis=-1, keepdims=True))
    return (grad_values, grad_gain)


def summed(parts):
    own, far, left, right = [part[...].astype(F32) for part in parts]
    return (own + far) + (left + right)


def fetch(mine, own, other, out, sem):
    @pl.when(mine)
    def _():
        pltpu.make_async_copy(own, out, sem).start()

    @pl.when(jnp.logical_not(mine))
    def _():
        pltpu.make_async_copy(other, out, sem).start()

    return pltpu.make_async_copy(own, out, sem)


def picked(mine, own, other):
    return jnp.where(mine, own[...].astype(F32), other[...].astype(F32))


def bucket_of_lane():
    offset = (128 - iota((128, 128), 1)) & 127
    return ones_where(jnp.minimum(offset, 31) == iota((128, 128), 0)).astype(BF16)


def head_mask(head):
    lane = iota((128, 3 * HEAD_DIM), 1)
    return (lane >= head * HEAD_DIM) & (lane < (head + 1) * HEAD_DIM)


def gelu_both(pre):
    inner = 0.7978845608028654
    cube = 0.044715
    square = pre * pre
    slope = jnp.tanh(inner * pre * (1.0 + cube * square))
    half = 0.5 * (1.0 + slope)
    value = pre * half
    grad = half + 0.5 * pre * (1.0 - slope * slope) * inner * (1.0 + 3.0 * cube * square)
    return (value, grad)


def attend_forward_kernel(
    chained,
    flag,
    *refs,
):
    mine = flag[0] == 1
    if chained:
        middle, own, far, left, right = refs[:5]
        refs = refs[5:]
    else:
        source = refs[0]
        refs = refs[1:]
    small_own, small_other, w_own, w_other, o_own, o_other = refs[:6]
    low, normed_ref, heads_ref, probs_ref, mixed_ref, part_ref = refs[6:12]
    w, o, sems = refs[12:]
    get_w = fetch(mine, w_own, w_other, w, sems.at[0])
    get_o = fetch(mine, o_own, o_other, o, sems.at[1])
    if chained:
        low[...] = (middle[...] + summed((own, far, left, right))).astype(BF16)
    else:
        low[...] = source[...]
    values = low[...].astype(F32)
    small = picked(mine, small_own, small_other)
    normed = (values * norm_scale(values) * small[GAIN_A : GAIN_A + 1]).astype(BF16)
    normed_ref[...] = normed
    table = small[TABLE : TABLE + 8, :128].astype(BF16)
    levels = nn(table, bucket_of_lane())
    causal = iota((128, 128), 0) >= iota((128, 128), 1)
    get_w.wait()
    query, key, value = [nn(normed, w[k]) for k in range(3)]
    key, value = key.astype(BF16), value.astype(BF16)
    heads_ref[0] = query.astype(BF16)
    heads_ref[1] = key
    heads_ref[2] = value
    query = heads_ref[0].astype(F32)
    mixed = jnp.zeros((128, 3 * HEAD_DIM), F32)
    for head in range(3):
        mask = head_mask(head)
        bias = pltpu.roll(
            jnp.broadcast_to(levels[head : head + 1], (128, 128)), 0, 1, stride=1, stride_axis=0
        )
        scores = nt(jnp.where(mask, query, 0.0).astype(BF16), key) * HEAD_DIM ** (-0.5) + bias
        scores = jnp.where(causal, scores, NEG)
        weights = jnp.exp(scores - jnp.max(scores, axis=-1, keepdims=True))
        probs = weights / jnp.sum(weights, axis=-1, keepdims=True)
        probs_ref[head] = probs
        mixed = jnp.where(mask, nn(probs.astype(BF16), value), mixed)
    mixed_ref[...] = mixed.astype(BF16)
    get_o.wait()
    part_ref[...] = nn(mixed_ref[...], o[...]).astype(BF16)


def dispatch_kernel(
    both,
    flag,
    low,
    own,
    far,
    left,
    right,
    small_own,
    small_other,
    routes,
    *refs,
):
    if both:
        cotangent = refs[0]
        refs = refs[1:]
    middle_ref, normed_ref, gates_ref, mix_ref, rest_ref, gap_ref, take_ref, buffer_ref = refs[:8]
    mine = flag[0] == 1
    middle = low[...].astype(F32) + summed((own, far, left, right))
    middle_ref[...] = middle
    small = picked(mine, small_own, small_other)
    normed = (middle * norm_scale(middle) * small[GAIN_M : GAIN_M + 1]).astype(BF16)
    normed_ref[...] = normed
    logits = nt(normed, small[:32].astype(BF16))
    lane = iota((128, 32), 1)
    route = [routes[:, k : k + 1] for k in range(2)]
    pick = [ones_where(one == lane) for one in route]
    before = nn(
        ones_where(iota((128, 128), 1) < iota((128, 128), 0)).astype(BF16),
        (pick[0] + pick[1]).astype(BF16),
    )
    chosen = [jnp.sum(logits * one, axis=-1, keepdims=True) for one in pick]
    top = jnp.maximum(chosen[0], chosen[1])
    weights = [jnp.exp(one - top) for one in chosen]
    total = weights[0] + weights[1]
    gates = [one / total for one in weights]
    wide = iota((128, 128), 1)
    gates_ref[...] = jnp.where(wide == 0, gates[0], jnp.where(wide == 1, gates[1], 0.0))
    place = [jnp.sum(before * one, axis=-1, keepdims=True).astype(jnp.int32) for one in pick]
    stride = 48 if both else 24
    slots = 16 * stride
    target = [(e >> 1) * stride + (e & 1) * 12 + at for e, at in zip(route, place)]
    slot = iota((128, slots), 1)
    mask = [ones_where(slot == one) for one in target]
    spread = mask[0] + mask[1]
    weighted = mask[0] * gates[0] + mask[1] * gates[1]
    high = weighted.astype(BF16)
    mix_ref[...] = high
    rest_ref[...] = (weighted - high.astype(F32)).astype(BF16)
    gap_ref[...] = (mask[0] - mask[1]).astype(BF16)
    buffer = nn(spread.T.astype(BF16), normed)
    if both:
        mask = [ones_where(slot == one + 24) for one in target]
        take_ref[...] = (mask[0] + mask[1]).astype(BF16)
        weighted = (mask[0] * gates[0] + mask[1] * gates[1]).T
        high = weighted.astype(BF16)
        rest = (weighted - high.astype(F32)).astype(BF16)
        buffer = buffer + (nn(high, cotangent[...]) + nn(rest, cotangent[...]))
    else:
        take_ref[...] = spread.astype(BF16)
    buffer_ref[...] = buffer.astype(BF16)


def raise_kernel(
    flag,
    raw,
    sort,
    unsort,
    up_own,
    up_other,
    down_own,
    down_other,
    arrived_ref,
    hidden_ref,
    slope_ref,
    rows_ref,
    up,
    down,
    rows,
    sems,
):
    mine = flag[0] == 1
    gets = [fetch(mine, up_own.at[e], up_other.at[e], up.at[e], sems.at[e]) for e in range(2)]
    gets += [fetch(mine, down_own.at[e], down_other.at[e], down.at[e], sems.at[2 + e]) for e in range(2)]
    arrived_ref[...] = nn(sort[...], raw[...]).astype(BF16)
    for e in range(2):
        part = pl.ds(192 * e, 192)
        gets[e].wait()
        value, slope = gelu_both(nn(arrived_ref[part, :], up[e]))
        hidden_ref[part, :] = value.astype(BF16)
        slope_ref[part, :] = slope.astype(BF16)
        gets[2 + e].wait()
        rows[part, :] = nn(hidden_ref[part, :], down[e]).astype(BF16)
    rows_ref[...] = nn(unsort[...], rows[...]).astype(BF16)


def lower_kernel(
    flag,
    raw,
    sort,
    unsort,
    arrived,
    hidden,
    slope,
    up_own,
    up_other,
    down_own,
    down_other,
    acts_ref,
    rows_ref,
    up,
    down,
    rows,
    sems,
):
    mine = flag[0] == 1
    gets = [fetch(mine, down_own.at[e], down_other.at[e], down.at[e], sems.at[2 + e]) for e in range(2)]
    gets += [fetch(mine, up_own.at[e], up_other.at[e], up.at[e], sems.at[e]) for e in range(2)]
    acts_ref[0] = hidden[...]
    acts_ref[2] = arrived[...]
    acts_ref[1] = nn(sort[...], raw[...]).astype(BF16)
    for e in range(2):
        part = pl.ds(192 * e, 192)
        gets[e].wait()
        grad_hidden = nt(acts_ref[1, part, :], down[e])
        acts_ref[3, part, :] = (slope[part, :].astype(F32) * grad_hidden).astype(BF16)
        gets[2 + e].wait()
        rows[part, :] = nt(acts_ref[3, part, :], up[e]).astype(BF16)
    rows_ref[...] = nn(unsort[...], rows[...]).astype(BF16)


def raise_lower_kernel(
    flag,
    raw,
    sort,
    unsort,
    up_own,
    up_other,
    down_own,
    down_other,
    acts_ref,
    rows_ref,
    up,
    down,
    rows,
    sems,
):
    mine = flag[0] == 1
    gets = [fetch(mine, up_own.at[e], up_other.at[e], up.at[e], sems.at[e]) for e in range(2)]
    gets += [fetch(mine, down_own.at[e], down_other.at[e], down.at[e], sems.at[2 + e]) for e in range(2)]
    both = nn(sort[...], raw[...]).astype(BF16)
    acts_ref[2] = both[:384]
    acts_ref[1] = both[384:]
    for e in range(2):
        part = pl.ds(192 * e, 192)
        behind = pl.ds(384 + 192 * e, 192)
        gets[e].wait()
        value, slope = gelu_both(nn(acts_ref[2, part, :], up[e]))
        acts_ref[0, part, :] = value.astype(BF16)
        gets[2 + e].wait()
        rows[part, :] = nn(acts_ref[0, part, :], down[e]).astype(BF16)
        grad_hidden = nt(acts_ref[1, part, :], down[e])
        acts_ref[3, part, :] = (slope * grad_hidden).astype(BF16)
        rows[behind, :] = nt(acts_ref[3, part, :], up[e]).astype(BF16)
    rows_ref[...] = nn(unsort[...], rows[...]).astype(BF16)


def combine_kernel(returned, mix, rest, gap, part_ref, gap_ref):
    rows = returned[...]
    part_ref[...] = (nn(mix[...], rows) + nn(rest[...], rows)).astype(BF16)
    gap_ref[...] = nn(gap[...], rows)


def side_columns(difference):
    lane = iota((128, 128), 1)
    high = difference.astype(BF16).astype(F32)
    return jnp.where(lane == 0, high, jnp.where(lane == 1, difference - high, 0.0)).astype(BF16)


def combine_back_kernel(returned, take, gap, low, part_ref):
    part_ref[:, :768] = nn(take[...], returned[...]).astype(BF16)
    difference = jnp.sum(low[...].astype(F32) * gap[...], axis=-1, keepdims=True)
    part_ref[:, 768:] = side_columns(difference)


def combine_both_kernel(returned, mix, rest, gap, take, low, part_ref, out_ref):
    rows = returned[...]
    part_ref[:, :768] = nn(take[...], rows).astype(BF16)
    difference = jnp.sum(low[...].astype(F32) * nn(gap[...], rows), axis=-1, keepdims=True)
    part_ref[:, 768:] = side_columns(difference)
    out_ref[...] = (nn(mix[...], rows) + nn(rest[...], rows)).astype(BF16)


def attend_backward_kernel(
    flag,
    own,
    far,
    left,
    right,
    gates,
    routes,
    normed_m,
    middle,
    low,
    small_own,
    small_other,
    normed_a,
    heads,
    probs,
    mixed,
    w_own,
    w_other,
    o_own,
    o_other,
    part_ref,
    middle_ref,
    acts_ref,
    w,
    o,
    sems,
):
    mine = flag[0] == 1
    get_o = fetch(mine, o_own, o_other, o, sems.at[1])
    get_w = fetch(mine, w_own, w_other, w, sems.at[0])
    total = summed((own, far, left, right))
    small = picked(mine, small_own, small_other)
    grad_normed = total[:, :768]
    difference = total[:, 768:769] + total[:, 769:770]
    grad_first = gates[:, 0:1] * gates[:, 1:2] * difference
    lane = iota((128, 128), 1)
    sign = ones_where(routes[:, 0:1] == lane) - ones_where(routes[:, 1:2] == lane)
    grad_logits = (grad_first * sign).astype(BF16).astype(F32)
    grad_router = nn(grad_logits.T.astype(BF16), normed_m[...])
    grad_normed = grad_normed + nn(grad_logits[:, :32].astype(BF16), small[:32].astype(BF16))
    grad_out = low[...].astype(F32)
    values = middle[...]
    grad_values, grad_gain = norm_back(
        grad_normed, values, norm_scale(values), small[GAIN_M : GAIN_M + 1]
    )
    grad_middle = grad_out + grad_values
    middle_ref[...] = grad_middle
    grad_attn = grad_middle.astype(BF16)
    acts_ref[128:256, :] = normed_a[...]
    acts_ref[256:384, :] = grad_attn
    get_o.wait()
    grad_mixed = nt(grad_attn, o[...]).astype(BF16)
    wide_mixed = grad_mixed.astype(F32)
    query, key, value = heads[0], heads[1], heads[2]
    zero = jnp.zeros((128, 3 * HEAD_DIM), F32)
    grads = [zero, zero, zero]
    turned = ones_where(iota((128, 128), 0) + iota((128, 128), 1) == 127).astype(BF16)
    levels = bucket_of_lane()
    tables = []
    for head in range(3):
        mask = head_mask(head)
        p = probs[head]
        grad_probs = nt(jnp.where(mask, wide_mixed, 0.0).astype(BF16), value)
        delta = jnp.sum(p * grad_probs, axis=-1, keepdims=True)
        grad_scores = (p * (grad_probs - delta)).astype(BF16)
        grads[0] = jnp.where(mask, nn(grad_scores, key), grads[0])
        grads[1] = jnp.where(mask, nn(flipped(grad_scores), query), grads[1])
        grads[2] = jnp.where(mask, nn(p.T.astype(BF16), grad_mixed), grads[2])
        skewed = pltpu.roll(nn(turned, grad_scores), 1, 1, stride=1, stride_axis=0)
        tables.append(jnp.sum(skewed, axis=0, keepdims=True))
    factor = HEAD_DIM ** (-0.5)
    grads = [(grads[0] * factor).astype(BF16), (grads[1] * factor).astype(BF16), grads[2].astype(BF16)]
    get_w.wait()
    part_ref[...] = (nt(grads[0], w[0]) + nt(grads[1], w[1]) + nt(grads[2], w[2])).astype(BF16)
    placed = jnp.zeros((128, 768), F32)
    away = iota((192, 768), 1) - iota((192, 768), 0)
    for k, one in enumerate(grads + [mixed[...]]):
        placed = placed + nn(one, ones_where(away == 192 * k).astype(BF16))
    acts_ref[:128, :] = placed.astype(BF16)
    row = iota((8, 128), 0)
    stacked = jnp.zeros((8, 128), F32)
    for head in range(3):
        stacked = jnp.where(row == 2 + head, tables[head], stacked)
    level_sums = lax.dot_general(
        stacked,
        levels.astype(F32),
        (((1,), (1,)), ((), ())),
        precision=lax.Precision.HIGHEST,
        preferred_element_type=F32,
    )
    row = iota((16, 768), 0)
    last = jnp.concatenate([level_sums, jnp.zeros((8, 640), F32)], axis=1)
    last = jnp.concatenate([last, jnp.zeros((8, 768), F32)], axis=0)
    last = jnp.where(row == 1, grad_gain, last)
    acts_ref[384:432, :] = jnp.concatenate([grad_router[:32], last], axis=0).astype(BF16)


def enter_kernel(chained, flag, own, far, left, right, grad_middle, low, small_own, small_other, *refs):
    mine = flag[0] == 1
    small = picked(mine, small_own, small_other)
    values = low[...].astype(F32)
    grad_values, grad_gain = norm_back(
        summed((own, far, left, right)), values, norm_scale(values), small[GAIN_A : GAIN_A + 1]
    )
    grad_in = grad_values + grad_middle[...]
    if chained:
        mix, rest, grad_ref, gain_ref, low_ref, buffer_ref = refs
        grad_low = grad_in.astype(BF16)
        low_ref[...] = grad_low
        buffer = nn(flipped(mix[...]), grad_low) + nn(flipped(rest[...]), grad_low)
        buffer_ref[...] = buffer.astype(BF16)
    else:
        grad_ref, gain_ref = refs
    grad_ref[...] = grad_in
    gain_ref[...] = jnp.broadcast_to(grad_gain, (8, 768))


def expert_grads_kernel(flag, acts_0, acts_1, sent_0, sent_1, up_hbm, down_hbm, held, made, sems, out_sems):
    first = flag[0] == 1
    gets = {}
    for which in range(4):
        for e in range(2):
            part = pl.ds(192 * e, 192)
            gets[which, e] = [
                fetch(
                    first,
                    pair[0].at[which, part, :],
                    pair[1].at[which, part, :],
                    held.at[which, e, pl.ds(192 * side, 192), :],
                    sems.at[which, e, side],
                )
                for side, pair in enumerate(((acts_0, acts_1), (sent_0, sent_1)))
            ]
    puts = []
    for e in range(2):
        for index, (left, right, out) in enumerate(((0, 1, down_hbm), (2, 3, up_hbm))):
            for get in gets[left, e] + gets[right, e]:
                get.wait()
            made[2 * e + index] = tn(held[left, e], held[right, e])
            put = pltpu.make_async_copy(made.at[2 * e + index], out.at[e], out_sems.at[2 * e + index])
            put.start()
            puts.append(put)
    for put in puts:
        put.wait()


def attend_grads_kernel(flag, acts_0, acts_1, sent_0, sent_1, packed_ref):
    first = flag[0] == 1
    own = picked(first, acts_0, acts_1)
    other = picked(first, sent_0, sent_1)

    def turned(rows):
        return jnp.concatenate([own[rows].T, other[rows].T], axis=1).astype(BF16)

    def stacked(rows):
        return jnp.concatenate([own[rows], other[rows]], axis=0).astype(BF16)

    left = turned(slice(0, 128))
    packed_ref[:576, :768] = nn(left[:576], stacked(slice(128, 256))).astype(BF16)
    packed_ref[576:, :768] = nn(left[576:], stacked(slice(256, 384))).astype(BF16)
    small = (own[384:432] + other[384:432]).astype(BF16)
    for group in range(6):
        packed_ref[48 * group : 48 * (group + 1), 768:] = small[:, 128 * group : 128 * (group + 1)]
    packed_ref[288:, 768:] = jnp.zeros((480, 128), BF16)


def sum_shares_kernel(flag, parts, gain_0, gain_1, sent_0, sent_1, out_ref):
    first = flag[0] == 1
    total = parts[0].astype(F32)
    for source in range(1, 16):
        total = total + parts[source].astype(F32)
    gain = (picked(first, gain_0, gain_1) + picked(first, sent_0, sent_1))[0:1]
    row = iota((48, 128), 0)
    side = total[:, 768:]
    for group in range(6):
        side = jnp.where(row == 40 + group, gain[:, 128 * group : 128 * (group + 1)], side)
    for source in range(16):
        out_ref[source, :, :768] = total[:, :768].astype(BF16)
        out_ref[source, :, 768:] = side.astype(BF16)


def unpack_kernel(whole, proj_ref, out_ref, router_ref, gain_a_ref, gain_m_ref, table_ref):
    eye = ones_where(iota((768, 768), 0) == iota((768, 768), 1)).astype(BF16)
    for k in range(3):
        proj_ref[k] = nt(eye, whole[192 * k : 192 * (k + 1), :768])
    out_ref[...] = whole[576:, :768].astype(F32)
    gain = jnp.zeros((48, 128), F32)
    for source in range(16):
        block = whole[48 * source : 48 * (source + 1), 768:].astype(F32)
        gain = gain + block
        if source < 6:
            lanes = slice(128 * source, 128 * (source + 1))
            gain_m_ref[:, lanes] = block[33:34]
            turned = nt(eye[:128, :128], block.astype(BF16))
            router_ref[lanes, :] = turned[:, :32]
        if source == 0:
            table_ref[...] = block[34:37, :32]
    for group in range(6):
        gain_a_ref[:, 128 * group : 128 * (group + 1)] = gain[40 + group : 41 + group]


def swap(array):
    return lax.ppermute(array, "section", [(0, 1), (1, 0)])


def to_second(array):
    return lax.ppermute(array, "section", [(0, 1)])


def to_first(array):
    return lax.ppermute(array, "section", [(1, 0)])


def ring(array, axis, by):
    size = lax.axis_size(axis)
    return lax.ppermute(array, axis, [(i, (i + by) % size) for i in range(size)])


def with_others(part):
    return (part, ring(part, "head", 2), ring(part, "head", 1), ring(part, "head", -1))


def exchange(rows):
    blocks = rows.reshape(16, rows.shape[0] // 16, rows.shape[1])
    return lax.all_to_all(blocks, "expert", 0, 0, tiled=True).reshape(rows.shape)


def sorting(stride, offsets):
    blocks = []
    for offset in offsets:
        for expert in range(2):
            at = np.arange(16)[:, None] * stride + offset + expert * 12 + np.arange(12)[None]
            blocks.append(at.reshape(-1))
    at = np.concatenate(blocks)
    table = np.zeros((at.size, 16 * stride), np.float32)
    table[np.arange(at.size), at] = 1.0
    return table.astype(ml_dtypes.bfloat16)


def on_device(
    inputs,
    cotangent,
    routes,
    attend_gain,
    query_key_value,
    attend_out,
    position_bias,
    mixture_gain,
    router,
    expert_up,
    expert_down,
):
    core = lax.axis_index("section")
    first = core == 0
    flags = [(core == which).astype(jnp.int32).reshape(1) for which in range(2)]
    blank = jnp.zeros((7, 768), BF16)
    small = jnp.concatenate(
        [
            router[0].T,
            attend_gain,
            blank,
            mixture_gain,
            blank,
            jnp.pad(position_bias[0], ((0, 13), (0, 736))),
        ]
    )
    small = (small, swap(small))
    w = (query_key_value[0], swap(query_key_value[0]))
    o = (attend_out[0], swap(attend_out[0]))
    route_own = jnp.where(first, routes[0, 0], routes[0, 1])
    route_other = swap(jnp.where(first, routes[0, 1], routes[0, 0]))
    tiles = (jnp.where(first, route_own, route_other), jnp.where(first, route_other, route_own))
    up = (expert_up[0], swap(expert_up[0]))
    down = (expert_down[0], swap(expert_down[0]))
    cot = jnp.where(first, cotangent[0], cotangent[1])

    row16 = ((128, 768), BF16)
    row32 = ((128, 768), F32)
    dma = pltpu.SemaphoreType.DMA
    attend_scratch = (pltpu.VMEM((3, 768, 192), BF16), pltpu.VMEM((192, 768), BF16), dma((2,)))

    def attend_forward(which, sources):
        return call(
            functools.partial(attend_forward_kernel, which == 1),
            f"attend{which}",
            [row16, row16, ((3, 128, 192), BF16), ((3, 128, 128), F32), ((128, 192), BF16), row16],
            [SMEM] + [VMEM] * (len(sources) + 2) + [ANY] * 4,
            (flags[which], *sources, *small, *w, *o),
            attend_scratch,
        )

    def dispatch(which, low, parts, extra):
        slots = 384 * (1 + which)
        mask = ((128, slots), BF16)
        return call(
            functools.partial(dispatch_kernel, which == 1),
            f"dispatch{which}",
            [row32, row16, ((128, 128), F32), mask, mask, mask, mask, ((slots, 768), BF16)],
            [SMEM] + [VMEM] * (8 + len(extra)),
            (flags[which], low, *parts, *small, tiles[which], *extra),
        )

    def expert_scratch(count):
        return (
            pltpu.VMEM((2, 768, 768), BF16),
            pltpu.VMEM((2, 768, 768), BF16),
            pltpu.VMEM((count, 768), BF16),
            dma((4,)),
        )

    def attend_backward(which, parts, gates, normed_m, middle, low, saved):
        return call(
            attend_backward_kernel,
            f"attend_back{which}",
            [row16, row32, ((432, 768), BF16)],
            [SMEM] + [VMEM] * 15 + [ANY] * 4,
            (flags[which], *parts, gates, tiles[which], normed_m, middle, low, *small, *saved, *w, *o),
            attend_scratch,
        )

    low_0, normed_a0, heads_0, probs_0, mixed_0, part = attend_forward(
        0, (jnp.where(first, inputs[0], inputs[1]),)
    )
    middle_0, normed_m0, gates_0, mix_0, rest_0, gap_0, take_0, buffer = dispatch(
        0, low_0, with_others(part), ()
    )
    sort_0, sort_1 = sorting(24, (0,)), sorting(48, (0, 24))
    unsort_0, unsort_1 = sort_0.T.copy(), sort_1.T.copy()
    block = ((384, 768), BF16)
    arrived, hidden, slope, rows = call(
        raise_kernel,
        "raise0",
        [block, block, block, block],
        [SMEM] + [VMEM] * 3 + [ANY] * 4,
        (flags[0], exchange(buffer), sort_0, unsort_0, *up, *down),
        expert_scratch(384),
    )
    part, gap_0 = call(
        combine_kernel, "combine0", [row16, row32], [VMEM] * 4, (exchange(rows), mix_0, rest_0, gap_0)
    )

    low_1, normed_a1, heads_1, probs_1, mixed_1, part = attend_forward(
        1, (middle_0, *with_others(part))
    )
    middle_1, normed_m1, gates_1, mix_1, rest_1, gap_1, take_1, buffer = dispatch(
        1, low_1, with_others(part), (cot,)
    )
    acts_ffn1, rows = call(
        raise_lower_kernel,
        "raise_lower1",
        [((4, 384, 768), BF16), ((768, 768), BF16)],
        [SMEM] + [VMEM] * 3 + [ANY] * 4,
        (flags[1], exchange(buffer), sort_1, unsort_1, *up, *down),
        expert_scratch(768),
    )
    part, part_out = call(
        combine_both_kernel,
        "combine1",
        [((128, 896), BF16), row16],
        [VMEM] * 6,
        (exchange(rows), mix_1, rest_1, gap_1, take_1, cot),
    )
    part, grad_middle, acts_1 = attend_backward(
        1, with_others(part), gates_1, normed_m1, middle_1, cot, (normed_a1, heads_1, probs_1, mixed_1)
    )
    mask = [SMEM] + [VMEM] * 8
    grad_1, gain_1, grad_low, buffer = call(
        functools.partial(enter_kernel, True),
        "enter1",
        [row32, ((8, 768), F32), row16, block],
        mask + [VMEM] * 2,
        (flags[1], *with_others(part), grad_middle, low_1, *small, mix_0, rest_0),
    )

    acts_ffn0, rows = call(
        lower_kernel,
        "lower0",
        [((4, 384, 768), BF16), block],
        [SMEM] + [VMEM] * 6 + [ANY] * 4,
        (flags[0], exchange(buffer), sort_0, unsort_0, arrived, hidden, slope, *up, *down),
        expert_scratch(384),
    )
    (part,) = call(
        combine_back_kernel,
        "combine_back0",
        [((128, 896), BF16)],
        [VMEM] * 4,
        (exchange(rows), take_0, gap_0, grad_low),
    )
    part, grad_middle, acts_0 = attend_backward(
        0, with_others(part), gates_0, normed_m0, middle_0, grad_low, (normed_a0, heads_0, probs_0, mixed_0)
    )
    (packed,) = call(
        attend_grads_kernel,
        "attend_grads",
        [((768, 896), BF16)],
        [SMEM] + [VMEM] * 4,
        (flags[0], acts_0, acts_1, to_first(acts_0), to_second(acts_1)),
    )
    shares = exchange(packed)
    grad_0, gain_0 = call(
        functools.partial(enter_kernel, False),
        "enter0",
        [row32, ((8, 768), F32)],
        mask,
        (flags[0], *with_others(part), grad_middle, low_0, *small),
    )
    (shares,) = call(
        sum_shares_kernel,
        "sum_shares",
        [((16, 48, 896), BF16)],
        [SMEM] + [VMEM] * 5,
        (flags[0], shares.reshape(16, 48, 896), gain_0, gain_1, to_first(gain_0), to_second(gain_1)),
    )
    grad_proj, grad_out, grad_router, grad_gain_a, grad_gain_m, grad_table = call(
        unpack_kernel,
        "unpack",
        [
            ((3, 768, 192), F32),
            ((192, 768), F32),
            ((768, 32), F32),
            ((1, 768), F32),
            ((1, 768), F32),
            ((3, 32), F32),
        ],
        [VMEM],
        (exchange(shares.reshape(768, 896)),),
    )
    grad_up, grad_down = call(
        expert_grads_kernel,
        "expert_grads",
        [((2, 768, 768), F32), ((2, 768, 768), F32)],
        [SMEM] + [ANY] * 4,
        (flags[0], acts_ffn0, acts_ffn1, to_first(acts_ffn0), to_second(acts_ffn1)),
        (
            pltpu.VMEM((4, 2, 384, 768), BF16),
            pltpu.VMEM((4, 768, 768), F32),
            dma((4, 2, 2)),
            dma((4,)),
        ),
        [ANY] * 2,
        flops=4 * 10**9,
        size=20 * 2**20,
    )
    out_1 = (middle_1 + summed(with_others(part_out))).astype(BF16)
    section_output = jnp.stack(
        [jnp.where(first, low_1, to_second(out_1)), jnp.where(first, to_first(low_1), out_1)]
    )
    input_grad = jnp.stack(
        [jnp.where(first, grad_0, to_second(grad_1)), jnp.where(first, to_first(grad_0), grad_1)]
    )
    return (
        section_output[None],
        input_grad[None],
        grad_gain_a,
        grad_proj[None],
        grad_out[None],
        grad_table[None],
        grad_gain_m,
        grad_router[None],
        grad_up[None],
        grad_down[None],
    )


def solution(mesh):
    return jax.shard_map(
        on_device,
        mesh=mesh,
        in_specs=(
            P(None, "expert", None),
            P(None, "expert", None),
            P("section", None, "expert", None),
            P("section", None),
            P("section", None, None, "head"),
            P("section", "head", None),
            P("section", "head", None),
            P("section", None),
            P("section", None, None),
            P("section", "expert", None, "head"),
            P("section", "expert", "head", None),
        ),
        out_specs=(
            P("section", None, "expert", None),
            P("section", None, "expert", None),
            P("section", None),
            P("section", None, None, "head"),
            P("section", "head", None),
            P("section", "head", None),
            P("section", None),
            P("section", None, None),
            P("section", "expert", None, "head"),
            P("section", "expert", "head", None),
        ),
        check_vma=False,
    )
```

```python
import functools

import jax
import jax.numpy as jnp
import ml_dtypes
import numpy as np
from jax import lax
from jax.experimental import pallas as pl
from jax.experimental.pallas import tpu as pltpu
from jax.sharding import PartitionSpec as P

HEAD_DIM = 64
EPS = 1e-06
NEG = -1e30
F32 = jnp.float32
BF16 = jnp.bfloat16
GAIN_A, GAIN_M, TABLE, SMALL = 32, 40, 48, 64

VMEM = pl.BlockSpec(memory_space=pltpu.VMEM)
SMEM = pl.BlockSpec(memory_space=pltpu.SMEM)
ANY = pl.BlockSpec(memory_space=pl.ANY)


def call(kernel, name, out_shape, in_specs, args, scratch=(), out_specs=None, flops=10**9, size=2**20, limit=48):
    return pl.pallas_call(
        kernel,
        name=name,
        out_shape=[jax.ShapeDtypeStruct(shape, dtype) for shape, dtype in out_shape],
        in_specs=in_specs,
        out_specs=out_specs or [VMEM] * len(out_shape),
        scratch_shapes=list(scratch),
        compiler_params=pltpu.CompilerParams(vmem_limit_bytes=limit * 2**20),
        cost_estimate=pl.CostEstimate(flops=flops, bytes_accessed=size, transcendentals=0),
    )(*args)


def nn(a, b):
    return lax.dot_general(a, b, (((1,), (0,)), ((), ())), preferred_element_type=F32)


def nt(a, b):
    return lax.dot_general(a, b, (((1,), (1,)), ((), ())), preferred_element_type=F32)


def tn(a, b):
    return lax.dot_general(a, b, (((0,), (0,)), ((), ())), preferred_element_type=F32)


def iota(shape, dim):
    return lax.broadcasted_iota(jnp.int32, shape, dim)


def ones_where(mask):
    return jnp.where(mask, 1.0, 0.0)


def flipped(array):
    return array.astype(F32).T.astype(BF16)


def norm_scale(values):
    return lax.rsqrt(jnp.mean(values * values, axis=-1, keepdims=True) + EPS)


def norm_back(grad_normed, values, scale, gain):
    unit = values * scale
    grad_gain = jnp.sum(grad_normed * unit, axis=0, keepdims=True)
    grad_unit = grad_normed * gain
    grad_values = scale * (grad_unit - unit * jnp.mean(grad_unit * unit, axis=-1, keepdims=True))
    return (grad_values, grad_gain)


def summed(parts):
    own, far, left, right = [part[...].astype(F32) for part in parts]
    return (own + far) + (left + right)


def fetch(mine, own, other, out, sem):
    @pl.when(mine)
    def _():
        pltpu.make_async_copy(own, out, sem).start()

    @pl.when(jnp.logical_not(mine))
    def _():
        pltpu.make_async_copy(other, out, sem).start()

    return pltpu.make_async_copy(own, out, sem)


def picked(mine, own, other):
    return jnp.where(mine, own[...].astype(F32), other[...].astype(F32))


def route_columns(mine, own, other):
    rows = jnp.where(mine, own[...], other[...])
    eye = iota((128, 128), 0) == iota((128, 128), 1)
    return [jnp.sum(jnp.where(eye, rows[k : k + 1], 0), axis=-1, keepdims=True) for k in range(2)]


def bucket_of_lane():
    offset = (128 - iota((128, 128), 1)) & 127
    return ones_where(jnp.minimum(offset, 31) == iota((128, 128), 0)).astype(BF16)


def head_mask(head):
    lane = iota((128, 3 * HEAD_DIM), 1)
    return (lane >= head * HEAD_DIM) & (lane < (head + 1) * HEAD_DIM)


def gelu_both(pre):
    inner = 0.7978845608028654
    cube = 0.044715
    square = pre * pre
    slope = jnp.tanh(inner * pre * (1.0 + cube * square))
    half = 0.5 * (1.0 + slope)
    value = pre * half
    grad = half + 0.5 * pre * (1.0 - slope * slope) * inner * (1.0 + 3.0 * cube * square)
    return (value, grad)


def attend_forward_kernel(
    chained,
    flag,
    *refs,
):
    mine = flag[0] == 1
    if chained:
        middle, own, far, left, right = refs[:5]
        refs = refs[5:]
    else:
        source = refs[0]
        refs = refs[1:]
    small_own, small_other, w_own, w_other, o_own, o_other = refs[:6]
    low, normed_ref, heads_ref, probs_ref, mixed_ref, part_ref = refs[6:12]
    w, o, sems = refs[12:]
    get_w = fetch(mine, w_own, w_other, w, sems.at[0])
    get_o = fetch(mine, o_own, o_other, o, sems.at[1])
    if chained:
        low[...] = (middle[...] + summed((own, far, left, right))).astype(BF16)
    else:
        low[...] = picked(mine, source.at[0], source.at[1]).astype(BF16)
    values = low[...].astype(F32)
    small = picked(mine, small_own, small_other)
    normed = (values * norm_scale(values) * small[GAIN_A : GAIN_A + 1]).astype(BF16)
    normed_ref[...] = normed
    table = small[TABLE : TABLE + 8, :128].astype(BF16)
    levels = nn(table, bucket_of_lane())
    causal = iota((128, 128), 0) >= iota((128, 128), 1)
    get_w.wait()
    query, key, value = [nt(normed, w[k]) for k in range(3)]
    key, value = key.astype(BF16), value.astype(BF16)
    heads_ref[0] = query.astype(BF16)
    heads_ref[1] = key
    heads_ref[2] = value
    query = heads_ref[0].astype(F32)
    mixed = jnp.zeros((128, 3 * HEAD_DIM), F32)
    for head in range(3):
        mask = head_mask(head)
        bias = pltpu.roll(
            jnp.broadcast_to(levels[head : head + 1], (128, 128)), 0, 1, stride=1, stride_axis=0
        )
        scores = nt(jnp.where(mask, query, 0.0).astype(BF16), key) * HEAD_DIM ** (-0.5) + bias
        scores = jnp.where(causal, scores, NEG)
        weights = jnp.exp(scores - jnp.max(scores, axis=-1, keepdims=True))
        probs = weights / jnp.sum(weights, axis=-1, keepdims=True)
        probs_ref[head] = probs
        mixed = jnp.where(mask, nn(probs.astype(BF16), value), mixed)
    mixed_ref[...] = mixed.astype(BF16)
    get_o.wait()
    part_ref[...] = nn(mixed_ref[...], o[...]).astype(BF16)


def dispatch_kernel(
    both,
    flag,
    low,
    own,
    far,
    left,
    right,
    small_own,
    small_other,
    route_own,
    route_other,
    *refs,
):
    if both:
        cotangents, cotangent = refs[0], refs[-1]
        cotangent[...] = picked(flag[0] == 0, cotangents.at[0], cotangents.at[1]).astype(BF16)
        refs = refs[1:-1]
    middle_ref, normed_ref, gates_ref, mix_ref, rest_ref, gap_ref, take_ref, buffer_ref = refs[:8]
    mine = flag[0] == 1
    middle = low[...].astype(F32) + summed((own, far, left, right))
    middle_ref[...] = middle
    small = picked(mine, small_own, small_other)
    normed = (middle * norm_scale(middle) * small[GAIN_M : GAIN_M + 1]).astype(BF16)
    normed_ref[...] = normed
    logits = nt(normed, small[:32].astype(BF16))
    lane = iota((128, 32), 1)
    route = route_columns(mine, route_own, route_other)
    pick = [ones_where(one == lane) for one in route]
    before = nn(
        ones_where(iota((128, 128), 1) < iota((128, 128), 0)).astype(BF16),
        (pick[0] + pick[1]).astype(BF16),
    )
    chosen = [jnp.sum(logits * one, axis=-1, keepdims=True) for one in pick]
    top = jnp.maximum(chosen[0], chosen[1])
    weights = [jnp.exp(one - top) for one in chosen]
    total = weights[0] + weights[1]
    gates = [one / total for one in weights]
    wide = iota((128, 128), 1)
    gates_ref[...] = jnp.where(wide == 0, gates[0], jnp.where(wide == 1, gates[1], 0.0))
    place = [jnp.sum(before * one, axis=-1, keepdims=True).astype(jnp.int32) for one in pick]
    stride = 48 if both else 24
    slots = 16 * stride
    target = [(e >> 1) * stride + (e & 1) * 12 + at for e, at in zip(route, place)]
    slot = iota((128, slots), 1)
    mask = [ones_where(slot == one) for one in target]
    spread = mask[0] + mask[1]
    weighted = mask[0] * gates[0] + mask[1] * gates[1]
    high = weighted.astype(BF16)
    mix_ref[...] = high
    rest_ref[...] = (weighted - high.astype(F32)).astype(BF16)
    gap_ref[...] = (mask[0] - mask[1]).astype(BF16)
    buffer = nn(spread.T.astype(BF16), normed)
    if both:
        mask = [ones_where(slot == one + 24) for one in target]
        take_ref[...] = (mask[0] + mask[1]).astype(BF16)
        weighted = (mask[0] * gates[0] + mask[1] * gates[1]).T
        high = weighted.astype(BF16)
        rest = (weighted - high.astype(F32)).astype(BF16)
        buffer = buffer + (nn(high, cotangent[...]) + nn(rest, cotangent[...]))
    else:
        take_ref[...] = spread.astype(BF16)
    buffer_ref[...] = buffer.astype(BF16)


def raise_kernel(
    flag,
    raw,
    sort,
    unsort,
    up_own,
    up_other,
    down_own,
    down_other,
    arrived_ref,
    hidden_ref,
    slope_ref,
    rows_ref,
    up,
    down,
    rows,
    sems,
):
    mine = flag[0] == 1
    gets = [fetch(mine, up_own.at[e], up_other.at[e], up.at[e], sems.at[e]) for e in range(2)]
    gets += [fetch(mine, down_own.at[e], down_other.at[e], down.at[e], sems.at[2 + e]) for e in range(2)]
    arrived_ref[...] = nn(sort[...], raw[...]).astype(BF16)
    for e in range(2):
        part = pl.ds(192 * e, 192)
        gets[e].wait()
        value, slope = gelu_both(nn(arrived_ref[part, :], up[e]))
        hidden_ref[part, :] = value.astype(BF16)
        slope_ref[part, :] = slope.astype(BF16)
        gets[2 + e].wait()
        rows[part, :] = nn(hidden_ref[part, :], down[e]).astype(BF16)
    rows_ref[...] = nn(unsort[...], rows[...]).astype(BF16)


def lower_kernel(
    flag,
    raw,
    sort,
    unsort,
    arrived,
    hidden,
    slope,
    up_own,
    up_other,
    down_own,
    down_other,
    acts_ref,
    rows_ref,
    up,
    down,
    rows,
    sems,
):
    mine = flag[0] == 1
    gets = [fetch(mine, down_own.at[e], down_other.at[e], down.at[e], sems.at[2 + e]) for e in range(2)]
    gets += [fetch(mine, up_own.at[e], up_other.at[e], up.at[e], sems.at[e]) for e in range(2)]
    acts_ref[0:384, :] = hidden[...]
    acts_ref[768:1152, :] = arrived[...]
    acts_ref[384:768, :] = nn(sort[...], raw[...]).astype(BF16)
    for e in range(2):
        part = pl.ds(192 * e, 192)
        gets[e].wait()
        grad_hidden = nt(acts_ref[pl.ds(384 + 192 * e, 192), :], down[e])
        acts_ref[pl.ds(1152 + 192 * e, 192), :] = (slope[part, :].astype(F32) * grad_hidden).astype(BF16)
        gets[2 + e].wait()
        rows[part, :] = nt(acts_ref[pl.ds(1152 + 192 * e, 192), :], up[e]).astype(BF16)
    rows_ref[...] = nn(unsort[...], rows[...]).astype(BF16)


def raise_lower_kernel(
    flag,
    raw,
    sort,
    unsort,
    up_own,
    up_other,
    down_own,
    down_other,
    acts_ref,
    rows_ref,
    up,
    down,
    rows,
    sems,
):
    mine = flag[0] == 1
    gets = [fetch(mine, up_own.at[e], up_other.at[e], up.at[e], sems.at[e]) for e in range(2)]
    gets += [fetch(mine, down_own.at[e], down_other.at[e], down.at[e], sems.at[2 + e]) for e in range(2)]
    both = nn(sort[...], raw[...]).astype(BF16)
    acts_ref[768:1152, :] = both[:384]
    acts_ref[384:768, :] = both[384:]
    for e in range(2):
        part = pl.ds(192 * e, 192)
        behind = pl.ds(384 + 192 * e, 192)
        gets[e].wait()
        value, slope = gelu_both(nn(acts_ref[pl.ds(768 + 192 * e, 192), :], up[e]))
        acts_ref[part, :] = value.astype(BF16)
        gets[2 + e].wait()
        rows[part, :] = nn(acts_ref[part, :], down[e]).astype(BF16)
        grad_hidden = nt(acts_ref[pl.ds(384 + 192 * e, 192), :], down[e])
        acts_ref[pl.ds(1152 + 192 * e, 192), :] = (slope * grad_hidden).astype(BF16)
        rows[behind, :] = nt(acts_ref[pl.ds(1152 + 192 * e, 192), :], up[e]).astype(BF16)
    rows_ref[...] = nn(unsort[...], rows[...]).astype(BF16)


def combine_kernel(returned, mix, rest, gap, part_ref, gap_ref):
    rows = returned[...]
    part_ref[...] = (nn(mix[...], rows) + nn(rest[...], rows)).astype(BF16)
    gap_ref[...] = nn(gap[...], rows)


def side_columns(difference):
    lane = iota((128, 128), 1)
    high = difference.astype(BF16).astype(F32)
    return jnp.where(lane == 0, high, jnp.where(lane == 1, difference - high, 0.0)).astype(BF16)


def combine_back_kernel(returned, take, gap, low, part_ref):
    part_ref[:, :768] = nn(take[...], returned[...]).astype(BF16)
    difference = jnp.sum(low[...].astype(F32) * gap[...], axis=-1, keepdims=True)
    part_ref[:, 768:] = side_columns(difference)


def combine_both_kernel(returned, mix, rest, gap, take, low, part_ref, out_ref):
    rows = returned[...]
    part_ref[:, :768] = nn(take[...], rows).astype(BF16)
    difference = jnp.sum(low[...].astype(F32) * nn(gap[...], rows), axis=-1, keepdims=True)
    part_ref[:, 768:] = side_columns(difference)
    out_ref[...] = (nn(mix[...], rows) + nn(rest[...], rows)).astype(BF16)


def attend_backward_kernel(
    flag,
    own,
    far,
    left,
    right,
    gates,
    route_own,
    route_other,
    normed_m,
    middle,
    low,
    small_own,
    small_other,
    normed_a,
    heads,
    probs,
    mixed,
    w_own,
    w_other,
    o_own,
    o_other,
    *refs,
):
    part_ref, middle_ref, acts_ref, w, o, sems = refs
    mine = flag[0] == 1
    get_o = fetch(mine, o_own, o_other, o, sems.at[1])
    get_w = fetch(mine, w_own, w_other, w, sems.at[0])
    total = summed((own, far, left, right))
    small = picked(mine, small_own, small_other)
    grad_normed = total[:, :768]
    difference = total[:, 768:769] + total[:, 769:770]
    grad_first = gates[:, 0:1] * gates[:, 1:2] * difference
    lane = iota((128, 128), 1)
    route = route_columns(mine, route_own, route_other)
    sign = ones_where(route[0] == lane) - ones_where(route[1] == lane)
    grad_logits = (grad_first * sign).astype(BF16).astype(F32)
    grad_router = nn(grad_logits.T.astype(BF16), normed_m[...])
    grad_normed = grad_normed + nn(grad_logits[:, :32].astype(BF16), small[:32].astype(BF16))
    grad_out = low[...].astype(F32)
    values = middle[...]
    grad_values, grad_gain = norm_back(
        grad_normed, values, norm_scale(values), small[GAIN_M : GAIN_M + 1]
    )
    grad_middle = grad_out + grad_values
    middle_ref[...] = grad_middle
    grad_attn = grad_middle.astype(BF16)
    acts_ref[128:256, :] = normed_a[...]
    acts_ref[256:384, :] = grad_attn
    get_o.wait()
    grad_mixed = nt(grad_attn, o[...]).astype(BF16)
    wide_mixed = grad_mixed.astype(F32)
    query, key, value = heads[0], heads[1], heads[2]
    zero = jnp.zeros((128, 3 * HEAD_DIM), F32)
    grads = [zero, zero, zero]
    turned = ones_where(iota((128, 128), 0) + iota((128, 128), 1) == 127).astype(BF16)
    levels = bucket_of_lane()
    tables = []
    for head in range(3):
        mask = head_mask(head)
        p = probs[head]
        grad_probs = nt(jnp.where(mask, wide_mixed, 0.0).astype(BF16), value)
        delta = jnp.sum(p * grad_probs, axis=-1, keepdims=True)
        grad_scores = (p * (grad_probs - delta)).astype(BF16)
        grads[0] = jnp.where(mask, nn(grad_scores, key), grads[0])
        grads[1] = jnp.where(mask, nn(flipped(grad_scores), query), grads[1])
        grads[2] = jnp.where(mask, nn(p.T.astype(BF16), grad_mixed), grads[2])
        skewed = pltpu.roll(nn(turned, grad_scores), 1, 1, stride=1, stride_axis=0)
        tables.append(jnp.sum(skewed, axis=0, keepdims=True))
    factor = HEAD_DIM ** (-0.5)
    grads = [(grads[0] * factor).astype(BF16), (grads[1] * factor).astype(BF16), grads[2].astype(BF16)]
    get_w.wait()
    part_ref[:128, :] = (nn(grads[0], w[0]) + nn(grads[1], w[1]) + nn(grads[2], w[2])).astype(BF16)
    placed = jnp.zeros((128, 768), F32)
    away = iota((192, 768), 1) - iota((192, 768), 0)
    for k, one in enumerate(grads + [mixed[...]]):
        placed = placed + nn(one, ones_where(away == 192 * k).astype(BF16))
    acts_ref[:128, :] = placed.astype(BF16)
    row = iota((8, 128), 0)
    stacked = jnp.zeros((8, 128), F32)
    for head in range(3):
        stacked = jnp.where(row == 2 + head, tables[head], stacked)
    level_sums = lax.dot_general(
        stacked,
        levels.astype(F32),
        (((1,), (1,)), ((), ())),
        precision=lax.Precision.HIGHEST,
        preferred_element_type=F32,
    )
    row = iota((16, 768), 0)
    last = jnp.concatenate([level_sums, jnp.zeros((8, 640), F32)], axis=1)
    last = jnp.concatenate([last, jnp.zeros((8, 768), F32)], axis=0)
    last = jnp.where(row == 1, grad_gain, last)
    acts_ref[384:432, :] = jnp.concatenate([grad_router[:32], last], axis=0).astype(BF16)


def enter_kernel(chained, flag, own, far, left, right, grad_middle, low, small_own, small_other, *refs):
    mine = flag[0] == 1
    small = picked(mine, small_own, small_other)
    values = low[...].astype(F32)
    total = summed((own, far, left, right))
    grad_values, grad_gain = norm_back(
        total, values, norm_scale(values), small[GAIN_A : GAIN_A + 1]
    )
    grad_in = grad_values + grad_middle[...]
    grad_ref = refs[-1]
    grad_ref[...] = grad_in
    gain_row = jnp.broadcast_to(grad_gain, (16, 768))
    if chained:
        mix, rest, gain_ref, low_ref, buffer_ref, give_ref = refs[:-1]
        grad_low = grad_in.astype(BF16)
        low_ref[...] = grad_low
        buffer = nn(flipped(mix[...]), grad_low) + nn(flipped(rest[...]), grad_low)
        buffer_ref[...] = buffer.astype(BF16)
        gain_ref[...] = gain_row
        give_ref[...] = picked(mine, low, low_ref).astype(BF16)
    else:
        gain_1, gain_ref, give_ref = refs[:-1]
        give_ref[:128, :] = grad_in.astype(BF16)
        give_ref[128:, :] = jnp.where(mine, gain_1[...], gain_row).astype(BF16)
        gain_ref[...] = jnp.where(mine, gain_row, gain_1[...])


def expert_grads_kernel(
    flag, acts_0, acts_1, sent_0, sent_1, up_hbm, down_hbm, held, made, sems, out_sems
):
    first = flag[0] == 1
    gets = {}
    for which in range(4):
        for e in range(2):
            part = pl.ds(384 * which + 192 * e, 192)
            gets[which, e] = [
                fetch(
                    first,
                    pair[0].at[part, :],
                    pair[1].at[part, :],
                    held.at[which, e, pl.ds(192 * side, 192), :],
                    sems.at[which, e, side],
                )
                for side, pair in enumerate(((acts_0, acts_1), (sent_0, sent_1)))
            ]
    puts = []
    for e in range(2):
        for index, (left, right, out) in enumerate(((0, 1, down_hbm), (2, 3, up_hbm))):
            for get in gets[left, e] + gets[right, e]:
                get.wait()
            made[2 * e + index] = tn(held[left, e], held[right, e])
            put = pltpu.make_async_copy(made.at[2 * e + index], out.at[e], out_sems.at[2 * e + index])
            put.start()
            puts.append(put)
    for put in puts:
        put.wait()


def gain_rows(gain):
    row = iota((8, 128), 0)
    out = jnp.zeros((8, 128), F32)
    for group in range(6):
        out = jnp.where(row == group, gain[:, 128 * group : 128 * (group + 1)], out)
    return out


def attend_grads_kernel(flag, acts_0, acts_1, sent_0, sent_1, packed_ref):
    first = flag[0] == 1
    own = picked(first, acts_0, acts_1)
    other = picked(first, sent_0, sent_1)

    def stacked(rows):
        return jnp.concatenate([own[rows], other[rows]], axis=0)

    left = stacked(slice(0, 128)).T.astype(BF16)
    packed_ref[:576, :768] = nn(left[:576], stacked(slice(128, 256)).astype(BF16)).astype(BF16)
    packed_ref[576:, :768] = nn(left[576:], stacked(slice(256, 384)).astype(BF16)).astype(BF16)
    small = (own[384:432] + other[384:432]).astype(BF16)
    for group in range(6):
        packed_ref[48 * group : 48 * (group + 1), 768:] = small[:, 128 * group : 128 * (group + 1)]
    packed_ref[288:, 768:] = jnp.zeros((480, 128), BF16)


def sum_shares_kernel(parts, gain, taken, out_ref):
    total = parts[0].astype(F32)
    for source in range(1, 16):
        total = total + parts[source].astype(F32)
    rows = gain_rows(gain[0:1] + taken[...].astype(F32)[128:129])
    side = jnp.concatenate([total[:40, 768:], rows], axis=0)
    share = jnp.concatenate([total[:, :768], side], axis=1).astype(BF16)
    for source in range(16):
        out_ref[source] = share


def unpack_kernel(shares, proj_ref, out_ref, router_ref, gain_a_ref, gain_m_ref, table_ref):
    whole = shares[...].astype(F32)
    for k in range(3):
        proj_ref[k] = whole[192 * k : 192 * (k + 1), :768]
    out_ref[...] = whole[576:, :768]
    gain = jnp.zeros((8, 128), F32)
    for block in range(16):
        gain = gain + whole[48 * block + 40 : 48 * block + 48, 768:]
    for group in range(6):
        lanes = slice(128 * group, 128 * (group + 1))
        router_ref[:, lanes] = whole[48 * group : 48 * group + 32, 768:]
        gain_m_ref[:, lanes] = whole[48 * group + 33 : 48 * group + 34, 768:]
        gain_a_ref[:, lanes] = gain[group : group + 1]
    table_ref[...] = whole[34:37, 768:800]


def prepare_kernel(flag, router, gain_a, gain_m, table, routes, small_ref, own_ref, give_ref):
    first = flag[0] == 1
    small_ref[:32, :] = router[...]
    row = iota((16, 768), 0)
    gains = jnp.where(row == 0, gain_a[...].astype(F32), jnp.where(row == 8, gain_m[...].astype(F32), 0.0))
    small_ref[32:48, :] = gains.astype(BF16)
    wide = jnp.concatenate([table[...].astype(F32), jnp.zeros((13, 32), F32)], axis=0)
    place = ones_where(iota((32, 768), 0) == iota((32, 768), 1)).astype(BF16)
    small_ref[48:64, :] = nn(wide.astype(BF16), place).astype(BF16)
    own_ref[...] = jnp.where(first, routes[0], routes[1])
    give_ref[...] = jnp.where(first, routes[1], routes[0])


def swap(array):
    return lax.ppermute(array, "section", [(0, 1), (1, 0)])


def to_second(array):
    return lax.ppermute(array, "section", [(0, 1)])


def to_first(array):
    return lax.ppermute(array, "section", [(1, 0)])


def ring(array, axis, by):
    size = lax.axis_size(axis)
    return lax.ppermute(array, axis, [(i, (i + by) % size) for i in range(size)])


def with_others(part):
    return (part, ring(part, "head", 2), ring(part, "head", 1), ring(part, "head", -1))


def exchange(rows):
    blocks = rows.reshape(16, rows.shape[0] // 16, rows.shape[1])
    return lax.all_to_all(blocks, "expert", 0, 0, tiled=True).reshape(rows.shape)


def sorting(stride, offsets):
    blocks = []
    for offset in offsets:
        for expert in range(2):
            at = np.arange(16)[:, None] * stride + offset + expert * 12 + np.arange(12)[None]
            blocks.append(at.reshape(-1))
    at = np.concatenate(blocks)
    table = np.zeros((at.size, 16 * stride), np.float32)
    table[np.arange(at.size), at] = 1.0
    return table.astype(ml_dtypes.bfloat16)


def on_device(
    inputs,
    cotangent,
    routes,
    attend_gain,
    query_key_value,
    attend_out,
    position_bias,
    mixture_gain,
    router,
    expert_up,
    expert_down,
):
    core = lax.axis_index("section")
    first = core == 0
    flags = [(core == which).astype(jnp.int32).reshape(1) for which in range(2)]
    small, route_own, route_give = call(
        prepare_kernel,
        "prepare",
        [((SMALL, 768), BF16), ((2, 128), jnp.int32), ((2, 128), jnp.int32)],
        [SMEM] + [VMEM] * 5,
        (
            flags[0],
            router[0].T,
            attend_gain,
            mixture_gain,
            position_bias[0],
            routes[0].transpose(0, 2, 1),
        ),
        limit=60,
    )
    small = (small, swap(small))
    w = query_key_value[0].transpose(0, 2, 1)
    w = (w, swap(w))
    o = (attend_out[0], swap(attend_out[0]))
    tiles = (route_own, swap(route_give))
    up = (expert_up[0], swap(expert_up[0]))
    down = (expert_down[0], swap(expert_down[0]))

    row16 = ((128, 768), BF16)
    row32 = ((128, 768), F32)
    dma = pltpu.SemaphoreType.DMA
    attend_scratch = (pltpu.VMEM((3, 192, 768), BF16), pltpu.VMEM((192, 768), BF16), dma((2,)))

    def attend_forward(which, sources):
        return call(
            functools.partial(attend_forward_kernel, which == 1),
            f"attend{which}",
            [row16, row16, ((3, 128, 192), BF16), ((3, 128, 128), F32), ((128, 192), BF16), row16],
            [SMEM] + [VMEM] * (len(sources) + 2) + [ANY] * 4,
            (flags[which], *sources, *small, *w, *o),
            attend_scratch,
        )

    def dispatch(which, low, parts, extra):
        slots = 384 * (1 + which)
        mask = ((128, slots), BF16)
        return call(
            functools.partial(dispatch_kernel, which == 1),
            f"dispatch{which}",
            [row32, row16, ((128, 128), F32), mask, mask, mask, mask, ((slots, 768), BF16)]
            + [row16] * len(extra),
            [SMEM] + [VMEM] * (9 + len(extra)),
            (flags[which], low, *parts, *small, *tiles, *extra),
        )

    def expert_scratch(count):
        return (
            pltpu.VMEM((2, 768, 768), BF16),
            pltpu.VMEM((2, 768, 768), BF16),
            pltpu.VMEM((count, 768), BF16),
            dma((4,)),
        )

    def attend_backward(which, parts, gates, normed_m, middle, low, saved):
        return call(
            attend_backward_kernel,
            f"attend_back{which}",
            [row16, row32, ((432, 768), BF16)],
            [SMEM] + [VMEM] * 16 + [ANY] * 4,
            (flags[which], *parts, gates, *tiles, normed_m, middle, low, *small, *saved, *w, *o),
            attend_scratch,
        )

    low_0, normed_a0, heads_0, probs_0, mixed_0, part = attend_forward(
        0, (inputs,)
    )
    middle_0, normed_m0, gates_0, mix_0, rest_0, gap_0, take_0, buffer = dispatch(
        0, low_0, with_others(part), ()
    )
    sort_0, sort_1 = sorting(24, (0,)), sorting(48, (0, 24))
    unsort_0, unsort_1 = sort_0.T.copy(), sort_1.T.copy()
    block = ((384, 768), BF16)
    arrived, hidden, slope, rows = call(
        raise_kernel,
        "raise0",
        [block, block, block, block],
        [SMEM] + [VMEM] * 3 + [ANY] * 4,
        (flags[0], exchange(buffer), sort_0, unsort_0, *up, *down),
        expert_scratch(384),
    )
    part, gap_0 = call(
        combine_kernel, "combine0", [row16, row32], [VMEM] * 4, (exchange(rows), mix_0, rest_0, gap_0)
    )

    low_1, normed_a1, heads_1, probs_1, mixed_1, part = attend_forward(
        1, (middle_0, *with_others(part))
    )
    middle_1, normed_m1, gates_1, mix_1, rest_1, gap_1, take_1, buffer, cot = dispatch(
        1, low_1, with_others(part), (cotangent,)
    )
    acts_ffn1, rows = call(
        raise_lower_kernel,
        "raise_lower1",
        [((1536, 768), BF16), ((768, 768), BF16)],
        [SMEM] + [VMEM] * 3 + [ANY] * 4,
        (flags[1], exchange(buffer), sort_1, unsort_1, *up, *down),
        expert_scratch(768),
    )
    part, part_out = call(
        combine_both_kernel,
        "combine1",
        [((128, 896), BF16), row16],
        [VMEM] * 6,
        (exchange(rows), mix_1, rest_1, gap_1, take_1, cot),
    )
    part, grad_middle, acts_1 = attend_backward(
        1, with_others(part), gates_1, normed_m1, middle_1, cot, (normed_a1, heads_1, probs_1, mixed_1)
    )
    mask = [SMEM] + [VMEM] * 8
    gain = ((16, 768), F32)
    gain_1, grad_low, buffer, give, grad_1 = call(
        functools.partial(enter_kernel, True),
        "enter1",
        [gain, row16, block, row16, row32],
        mask + [VMEM] * 2,
        (flags[1], *with_others(part), grad_middle, low_1, *small, mix_0, rest_0),
    )
    taken_1 = swap(give)

    acts_ffn0, rows = call(
        lower_kernel,
        "lower0",
        [((1536, 768), BF16), block],
        [SMEM] + [VMEM] * 6 + [ANY] * 4,
        (flags[0], exchange(buffer), sort_0, unsort_0, arrived, hidden, slope, *up, *down),
        expert_scratch(384),
    )
    (part,) = call(
        combine_back_kernel,
        "combine_back0",
        [((128, 896), BF16)],
        [VMEM] * 4,
        (exchange(rows), take_0, gap_0, grad_low),
    )
    part, grad_middle, acts_0 = attend_backward(
        0, with_others(part), gates_0, normed_m0, middle_0, grad_low, (normed_a0, heads_0, probs_0, mixed_0)
    )
    (packed,) = call(
        attend_grads_kernel,
        "attend_grads",
        [((768, 896), BF16)],
        [SMEM] + [VMEM] * 4,
        (flags[0], acts_0, acts_1, to_first(acts_0), to_second(acts_1)),
    )
    packed, acts_ffn0, acts_ffn1 = lax.optimization_barrier((packed, acts_ffn0, acts_ffn1))
    shares = exchange(packed)
    gain_mine, give, grad_0 = call(
        functools.partial(enter_kernel, False),
        "enter0",
        [gain, ((144, 768), BF16), row32],
        mask + [VMEM],
        (flags[0], *with_others(part), grad_middle, low_0, *small, gain_1),
    )
    taken_0 = swap(give)
    grad_up, grad_down = call(
        expert_grads_kernel,
        "expert_grads",
        [((2, 768, 768), F32), ((2, 768, 768), F32)],
        [SMEM] + [ANY] * 4,
        (flags[0], acts_ffn0, acts_ffn1, to_first(acts_ffn0), to_second(acts_ffn1)),
        (
            pltpu.VMEM((4, 2, 384, 768), BF16),
            pltpu.VMEM((4, 768, 768), F32),
            dma((4, 2, 2)),
            dma((4,)),
        ),
        [ANY] * 2,
        flops=4 * 10**9,
        size=20 * 2**20,
    )
    (shares,) = call(
        sum_shares_kernel,
        "sum_shares",
        [((16, 48, 896), BF16)],
        [VMEM] * 3,
        (shares.reshape(16, 48, 896), gain_mine, taken_0),
    )
    shares, part_out = lax.optimization_barrier((shares, part_out))
    out_1 = (middle_1 + summed(with_others(part_out))).astype(BF16)
    grad_proj, grad_out, grad_router, grad_gain_a, grad_gain_m, grad_table = call(
        unpack_kernel,
        "unpack",
        [
            ((3, 192, 768), F32),
            ((192, 768), F32),
            ((32, 768), F32),
            ((1, 768), F32),
            ((1, 768), F32),
            ((3, 32), F32),
        ],
        [VMEM],
        (exchange(shares.reshape(768, 896)),),
    )
    taken_0 = taken_0[:128]
    section_output = jnp.stack(
        [jnp.where(first, low_1, to_second(out_1)), jnp.where(first, taken_1, out_1)]
    )
    input_grad = jnp.stack(
        [
            jnp.where(first, grad_0, taken_1.astype(F32)),
            jnp.where(first, taken_0.astype(F32), grad_1),
        ]
    )
    return (
        section_output[None],
        input_grad[None],
        grad_gain_a,
        grad_proj.transpose(0, 2, 1)[None],
        grad_out[None],
        grad_table[None],
        grad_gain_m,
        grad_router.T[None],
        grad_up[None],
        grad_down[None],
    )


def solution(mesh):
    return jax.shard_map(
        on_device,
        mesh=mesh,
        in_specs=(
            P(None, "expert", None),
            P(None, "expert", None),
            P("section", None, "expert", None),
            P("section", None),
            P("section", None, None, "head"),
            P("section", "head", None),
            P("section", "head", None),
            P("section", None),
            P("section", None, None),
            P("section", "expert", None, "head"),
            P("section", "expert", "head", None),
        ),
        out_specs=(
            P("section", None, "expert", None),
            P("section", None, "expert", None),
            P("section", None),
            P("section", None, None, "head"),
            P("section", "head", None),
            P("section", "head", None),
            P("section", None),
            P("section", None, None),
            P("section", "expert", None, "head"),
            P("section", "expert", "head", None),
        ),
        check_vma=False,
    )
```

```python
import functools

import jax
import jax.numpy as jnp
import ml_dtypes
import numpy as np
from jax import lax
from jax.experimental import pallas as pl
from jax.experimental.pallas import tpu as pltpu
from jax.sharding import PartitionSpec as P

HEAD_DIM = 64
EPS = 1e-06
NEG = -1e30
F32 = jnp.float32
BF16 = jnp.bfloat16
GAIN_A, GAIN_M, TABLE, SMALL = 32, 40, 48, 64

VMEM = pl.BlockSpec(memory_space=pltpu.VMEM)
SMEM = pl.BlockSpec(memory_space=pltpu.SMEM)
ANY = pl.BlockSpec(memory_space=pl.ANY)


def call(kernel, name, out_shape, in_specs, args, scratch=(), out_specs=None, flops=10**9, size=2**20, limit=48):
    return pl.pallas_call(
        kernel,
        name=name,
        out_shape=[jax.ShapeDtypeStruct(shape, dtype) for shape, dtype in out_shape],
        in_specs=in_specs,
        out_specs=out_specs or [VMEM] * len(out_shape),
        scratch_shapes=list(scratch),
        compiler_params=pltpu.CompilerParams(vmem_limit_bytes=limit * 2**20),
        cost_estimate=pl.CostEstimate(flops=flops, bytes_accessed=size, transcendentals=0),
    )(*args)


def nn(a, b):
    return lax.dot_general(a, b, (((1,), (0,)), ((), ())), preferred_element_type=F32)


def nt(a, b):
    return lax.dot_general(a, b, (((1,), (1,)), ((), ())), preferred_element_type=F32)


def tn(a, b):
    return lax.dot_general(a, b, (((0,), (0,)), ((), ())), preferred_element_type=F32)


def iota(shape, dim):
    return lax.broadcasted_iota(jnp.int32, shape, dim)


def ones_where(mask):
    return jnp.where(mask, 1.0, 0.0)


def flipped(array):
    return array.astype(F32).T.astype(BF16)


def norm_scale(values):
    return lax.rsqrt(jnp.mean(values * values, axis=-1, keepdims=True) + EPS)


def norm_back(grad_normed, values, scale, gain):
    unit = values * scale
    grad_gain = jnp.sum(grad_normed * unit, axis=0, keepdims=True)
    grad_unit = grad_normed * gain
    grad_values = scale * (grad_unit - unit * jnp.mean(grad_unit * unit, axis=-1, keepdims=True))
    return (grad_values, grad_gain)


def summed(parts):
    own, far, left, right = [part[...].astype(F32) for part in parts]
    return (own + far) + (left + right)


def fetch(mine, own, other, out, sem):
    @pl.when(mine)
    def _():
        pltpu.make_async_copy(own, out, sem).start()

    @pl.when(jnp.logical_not(mine))
    def _():
        pltpu.make_async_copy(other, out, sem).start()

    return pltpu.make_async_copy(own, out, sem)


def picked(mine, own, other):
    return jnp.where(mine, own[...].astype(F32), other[...].astype(F32))


def route_columns(mine, own, other):
    rows = jnp.where(mine, own[...], other[...])
    eye = iota((128, 128), 0) == iota((128, 128), 1)
    return [jnp.sum(jnp.where(eye, rows[k : k + 1], 0), axis=-1, keepdims=True) for k in range(2)]


def bucket_of_lane():
    offset = (128 - iota((128, 128), 1)) & 127
    return ones_where(jnp.minimum(offset, 31) == iota((128, 128), 0)).astype(BF16)


def head_mask(head):
    lane = iota((128, 3 * HEAD_DIM), 1)
    return (lane >= head * HEAD_DIM) & (lane < (head + 1) * HEAD_DIM)


def gelu_both(pre):
    inner = 0.7978845608028654
    cube = 0.044715
    square = pre * pre
    slope = jnp.tanh(inner * pre * (1.0 + cube * square))
    half = 0.5 * (1.0 + slope)
    value = pre * half
    grad = half + 0.5 * pre * (1.0 - slope * slope) * inner * (1.0 + 3.0 * cube * square)
    return (value, grad)


def attend_forward_kernel(
    chained,
    flag,
    *refs,
):
    mine = flag[0] == 1
    if chained:
        middle, own, far, left, right = refs[:5]
        refs = refs[5:]
    else:
        source = refs[0]
        refs = refs[1:]
    small_own, small_other, w_own, w_other, o_own, o_other = refs[:6]
    low, normed_ref, heads_ref, probs_ref, mixed_ref, part_ref = refs[6:12]
    w, o, sems = refs[12:]
    get_w = fetch(mine, w_own, w_other, w, sems.at[0])
    get_o = fetch(mine, o_own, o_other, o, sems.at[1])
    if chained:
        low[...] = (middle[...] + summed((own, far, left, right))).astype(BF16)
    else:
        low[...] = picked(mine, source.at[0], source.at[1]).astype(BF16)
    values = low[...].astype(F32)
    small = picked(mine, small_own, small_other)
    normed = (values * norm_scale(values) * small[GAIN_A : GAIN_A + 1]).astype(BF16)
    normed_ref[...] = normed
    table = small[TABLE : TABLE + 8, :128].astype(BF16)
    levels = nn(table, bucket_of_lane())
    causal = iota((128, 128), 0) >= iota((128, 128), 1)
    get_w.wait()
    query, key, value = [nt(normed, w[k]) for k in range(3)]
    key, value = key.astype(BF16), value.astype(BF16)
    heads_ref[0] = query.astype(BF16)
    heads_ref[1] = key
    heads_ref[2] = value
    query = heads_ref[0].astype(F32)
    mixed = jnp.zeros((128, 3 * HEAD_DIM), F32)
    for head in range(3):
        mask = head_mask(head)
        bias = pltpu.roll(
            jnp.broadcast_to(levels[head : head + 1], (128, 128)), 0, 1, stride=1, stride_axis=0
        )
        scores = nt(jnp.where(mask, query, 0.0).astype(BF16), key) * HEAD_DIM ** (-0.5) + bias
        scores = jnp.where(causal, scores, NEG)
        weights = jnp.exp(scores - jnp.max(scores, axis=-1, keepdims=True))
        probs = weights / jnp.sum(weights, axis=-1, keepdims=True)
        probs_ref[head] = probs
        mixed = jnp.where(mask, nn(probs.astype(BF16), value), mixed)
    mixed_ref[...] = mixed.astype(BF16)
    get_o.wait()
    part_ref[...] = nn(mixed_ref[...], o[...]).astype(BF16)


def dispatch_kernel(
    both,
    flag,
    low,
    own,
    far,
    left,
    right,
    small_own,
    small_other,
    route_own,
    route_other,
    *refs,
):
    if both:
        cotangents, cotangent = refs[0], refs[-1]
        cotangent[...] = picked(flag[0] == 0, cotangents.at[0], cotangents.at[1]).astype(BF16)
        refs = refs[1:-1]
    middle_ref, normed_ref, gates_ref, mix_ref, rest_ref, gap_ref, take_ref, buffer_ref = refs[:8]
    mine = flag[0] == 1
    middle = low[...].astype(F32) + summed((own, far, left, right))
    middle_ref[...] = middle
    small = picked(mine, small_own, small_other)
    normed = (middle * norm_scale(middle) * small[GAIN_M : GAIN_M + 1]).astype(BF16)
    normed_ref[...] = normed
    logits = nt(normed, small[:32].astype(BF16))
    lane = iota((128, 32), 1)
    route = route_columns(mine, route_own, route_other)
    pick = [ones_where(one == lane) for one in route]
    before = nn(
        ones_where(iota((128, 128), 1) < iota((128, 128), 0)).astype(BF16),
        (pick[0] + pick[1]).astype(BF16),
    )
    chosen = [jnp.sum(logits * one, axis=-1, keepdims=True) for one in pick]
    top = jnp.maximum(chosen[0], chosen[1])
    weights = [jnp.exp(one - top) for one in chosen]
    total = weights[0] + weights[1]
    gates = [one / total for one in weights]
    wide = iota((128, 128), 1)
    gates_ref[...] = jnp.where(wide == 0, gates[0], jnp.where(wide == 1, gates[1], 0.0))
    place = [jnp.sum(before * one, axis=-1, keepdims=True).astype(jnp.int32) for one in pick]
    stride = 48 if both else 24
    slots = 16 * stride
    target = [(e >> 1) * stride + (e & 1) * 12 + at for e, at in zip(route, place)]
    slot = iota((128, slots), 1)
    mask = [ones_where(slot == one) for one in target]
    spread = mask[0] + mask[1]
    weighted = mask[0] * gates[0] + mask[1] * gates[1]
    high = weighted.astype(BF16)
    mix_ref[...] = high
    rest_ref[...] = (weighted - high.astype(F32)).astype(BF16)
    gap_ref[...] = (mask[0] - mask[1]).astype(BF16)
    buffer = nn(spread.T.astype(BF16), normed)
    if both:
        mask = [ones_where(slot == one + 24) for one in target]
        take_ref[...] = (mask[0] + mask[1]).astype(BF16)
        weighted = (mask[0] * gates[0] + mask[1] * gates[1]).T
        high = weighted.astype(BF16)
        rest = (weighted - high.astype(F32)).astype(BF16)
        buffer = buffer + (nn(high, cotangent[...]) + nn(rest, cotangent[...]))
    else:
        take_ref[...] = spread.astype(BF16)
    buffer_ref[...] = buffer.astype(BF16)


def raise_kernel(
    flag,
    raw,
    sort,
    unsort,
    up_own,
    up_other,
    down_own,
    down_other,
    arrived_ref,
    hidden_ref,
    slope_ref,
    rows_ref,
    up,
    down,
    rows,
    sems,
):
    mine = flag[0] == 1
    gets = [fetch(mine, up_own.at[e], up_other.at[e], up.at[e], sems.at[e]) for e in range(2)]
    gets += [fetch(mine, down_own.at[e], down_other.at[e], down.at[e], sems.at[2 + e]) for e in range(2)]
    arrived_ref[...] = nn(sort[...], raw[...]).astype(BF16)
    for e in range(2):
        part = pl.ds(192 * e, 192)
        gets[e].wait()
        value, slope = gelu_both(nn(arrived_ref[part, :], up[e]))
        hidden_ref[part, :] = value.astype(BF16)
        slope_ref[part, :] = slope.astype(BF16)
        gets[2 + e].wait()
        rows[part, :] = nn(hidden_ref[part, :], down[e]).astype(BF16)
    rows_ref[...] = nn(unsort[...], rows[...]).astype(BF16)


def lower_kernel(
    flag,
    raw,
    sort,
    unsort,
    arrived,
    hidden,
    slope,
    up_own,
    up_other,
    down_own,
    down_other,
    acts_ref,
    rows_ref,
    up,
    down,
    rows,
    sems,
):
    mine = flag[0] == 1
    gets = [fetch(mine, down_own.at[e], down_other.at[e], down.at[e], sems.at[2 + e]) for e in range(2)]
    gets += [fetch(mine, up_own.at[e], up_other.at[e], up.at[e], sems.at[e]) for e in range(2)]
    acts_ref[0:384, :] = hidden[...]
    acts_ref[768:1152, :] = arrived[...]
    acts_ref[384:768, :] = nn(sort[...], raw[...]).astype(BF16)
    for e in range(2):
        part = pl.ds(192 * e, 192)
        gets[e].wait()
        grad_hidden = nt(acts_ref[pl.ds(384 + 192 * e, 192), :], down[e])
        acts_ref[pl.ds(1152 + 192 * e, 192), :] = (slope[part, :].astype(F32) * grad_hidden).astype(BF16)
        gets[2 + e].wait()
        rows[part, :] = nt(acts_ref[pl.ds(1152 + 192 * e, 192), :], up[e]).astype(BF16)
    rows_ref[...] = nn(unsort[...], rows[...]).astype(BF16)


def raise_lower_kernel(
    flag,
    raw,
    sort,
    unsort,
    up_own,
    up_other,
    down_own,
    down_other,
    acts_ref,
    rows_ref,
    up,
    down,
    rows,
    sems,
):
    mine = flag[0] == 1
    gets = [fetch(mine, up_own.at[e], up_other.at[e], up.at[e], sems.at[e]) for e in range(2)]
    gets += [fetch(mine, down_own.at[e], down_other.at[e], down.at[e], sems.at[2 + e]) for e in range(2)]
    both = nn(sort[...], raw[...]).astype(BF16)
    acts_ref[768:1152, :] = both[:384]
    acts_ref[384:768, :] = both[384:]
    for e in range(2):
        part = pl.ds(192 * e, 192)
        behind = pl.ds(384 + 192 * e, 192)
        gets[e].wait()
        value, slope = gelu_both(nn(acts_ref[pl.ds(768 + 192 * e, 192), :], up[e]))
        acts_ref[part, :] = value.astype(BF16)
        gets[2 + e].wait()
        rows[part, :] = nn(acts_ref[part, :], down[e]).astype(BF16)
        grad_hidden = nt(acts_ref[pl.ds(384 + 192 * e, 192), :], down[e])
        acts_ref[pl.ds(1152 + 192 * e, 192), :] = (slope * grad_hidden).astype(BF16)
        rows[behind, :] = nt(acts_ref[pl.ds(1152 + 192 * e, 192), :], up[e]).astype(BF16)
    rows_ref[...] = nn(unsort[...], rows[...]).astype(BF16)


def combine_kernel(returned, mix, rest, gap, part_ref, gap_ref):
    rows = returned[...]
    part_ref[...] = (nn(mix[...], rows) + nn(rest[...], rows)).astype(BF16)
    gap_ref[...] = nn(gap[...], rows)


def side_columns(difference):
    lane = iota((128, 128), 1)
    high = difference.astype(BF16).astype(F32)
    return jnp.where(lane == 0, high, jnp.where(lane == 1, difference - high, 0.0)).astype(BF16)


def combine_back_kernel(returned, take, gap, low, part_ref):
    part_ref[:, :768] = nn(take[...], returned[...]).astype(BF16)
    difference = jnp.sum(low[...].astype(F32) * gap[...], axis=-1, keepdims=True)
    part_ref[:, 768:] = side_columns(difference)


def combine_both_kernel(returned, mix, rest, gap, take, low, part_ref, out_ref):
    rows = returned[...]
    part_ref[:, :768] = nn(take[...], rows).astype(BF16)
    difference = jnp.sum(low[...].astype(F32) * nn(gap[...], rows), axis=-1, keepdims=True)
    part_ref[:, 768:] = side_columns(difference)
    out_ref[...] = (nn(mix[...], rows) + nn(rest[...], rows)).astype(BF16)


def attend_backward_kernel(
    flag,
    own,
    far,
    left,
    right,
    gates,
    route_own,
    route_other,
    normed_m,
    middle,
    low,
    small_own,
    small_other,
    normed_a,
    heads,
    probs,
    mixed,
    w_own,
    w_other,
    o_own,
    o_other,
    *refs,
):
    part_ref, middle_ref, acts_ref, w, o, sems = refs
    mine = flag[0] == 1
    get_o = fetch(mine, o_own, o_other, o, sems.at[1])
    get_w = fetch(mine, w_own, w_other, w, sems.at[0])
    total = summed((own, far, left, right))
    small = picked(mine, small_own, small_other)
    grad_normed = total[:, :768]
    difference = total[:, 768:769] + total[:, 769:770]
    grad_first = gates[:, 0:1] * gates[:, 1:2] * difference
    lane = iota((128, 128), 1)
    route = route_columns(mine, route_own, route_other)
    sign = ones_where(route[0] == lane) - ones_where(route[1] == lane)
    grad_logits = (grad_first * sign).astype(BF16).astype(F32)
    grad_router = nn(grad_logits.T.astype(BF16), normed_m[...])
    grad_normed = grad_normed + nn(grad_logits[:, :32].astype(BF16), small[:32].astype(BF16))
    grad_out = low[...].astype(F32)
    values = middle[...]
    grad_values, grad_gain = norm_back(
        grad_normed, values, norm_scale(values), small[GAIN_M : GAIN_M + 1]
    )
    grad_middle = grad_out + grad_values
    middle_ref[...] = grad_middle
    grad_attn = grad_middle.astype(BF16)
    acts_ref[128:256, :] = normed_a[...]
    acts_ref[256:384, :] = grad_attn
    get_o.wait()
    grad_mixed = nt(grad_attn, o[...]).astype(BF16)
    wide_mixed = grad_mixed.astype(F32)
    query, key, value = heads[0], heads[1], heads[2]
    zero = jnp.zeros((128, 3 * HEAD_DIM), F32)
    grads = [zero, zero, zero]
    turned = ones_where(iota((128, 128), 0) + iota((128, 128), 1) == 127).astype(BF16)
    levels = bucket_of_lane()
    tables = []
    for head in range(3):
        mask = head_mask(head)
        p = probs[head]
        grad_probs = nt(jnp.where(mask, wide_mixed, 0.0).astype(BF16), value)
        delta = jnp.sum(p * grad_probs, axis=-1, keepdims=True)
        grad_scores = (p * (grad_probs - delta)).astype(BF16)
        grads[0] = jnp.where(mask, nn(grad_scores, key), grads[0])
        grads[1] = jnp.where(mask, nn(flipped(grad_scores), query), grads[1])
        grads[2] = jnp.where(mask, nn(p.T.astype(BF16), grad_mixed), grads[2])
        skewed = pltpu.roll(nn(turned, grad_scores), 1, 1, stride=1, stride_axis=0)
        tables.append(jnp.sum(skewed, axis=0, keepdims=True))
    factor = HEAD_DIM ** (-0.5)
    grads = [(grads[0] * factor).astype(BF16), (grads[1] * factor).astype(BF16), grads[2].astype(BF16)]
    get_w.wait()
    part_ref[:128, :] = (nn(grads[0], w[0]) + nn(grads[1], w[1]) + nn(grads[2], w[2])).astype(BF16)
    placed = jnp.zeros((128, 768), F32)
    away = iota((192, 768), 1) - iota((192, 768), 0)
    for k, one in enumerate(grads + [mixed[...]]):
        placed = placed + nn(one, ones_where(away == 192 * k).astype(BF16))
    acts_ref[:128, :] = placed.astype(BF16)
    row = iota((8, 128), 0)
    stacked = jnp.zeros((8, 128), F32)
    for head in range(3):
        stacked = jnp.where(row == 2 + head, tables[head], stacked)
    level_sums = lax.dot_general(
        stacked,
        levels.astype(F32),
        (((1,), (1,)), ((), ())),
        precision=lax.Precision.HIGHEST,
        preferred_element_type=F32,
    )
    row = iota((16, 768), 0)
    last = jnp.concatenate([level_sums, jnp.zeros((8, 640), F32)], axis=1)
    last = jnp.concatenate([last, jnp.zeros((8, 768), F32)], axis=0)
    last = jnp.where(row == 1, grad_gain, last)
    acts_ref[384:432, :] = jnp.concatenate([grad_router[:32], last], axis=0).astype(BF16)


def enter_kernel(chained, flag, own, far, left, right, grad_middle, low, small_own, small_other, *refs):
    mine = flag[0] == 1
    small = picked(mine, small_own, small_other)
    values = low[...].astype(F32)
    total = summed((own, far, left, right))
    grad_values, grad_gain = norm_back(
        total, values, norm_scale(values), small[GAIN_A : GAIN_A + 1]
    )
    grad_in = grad_values + grad_middle[...]
    grad_ref = refs[-1]
    grad_ref[...] = grad_in
    gain_row = jnp.broadcast_to(grad_gain, (16, 768))
    if chained:
        mix, rest, gain_ref, low_ref, buffer_ref, give_ref = refs[:-1]
        grad_low = grad_in.astype(BF16)
        low_ref[...] = grad_low
        buffer = nn(flipped(mix[...]), grad_low) + nn(flipped(rest[...]), grad_low)
        buffer_ref[...] = buffer.astype(BF16)
        gain_ref[...] = gain_row
        give_ref[...] = picked(mine, low, low_ref).astype(BF16)
    else:
        gain_1, gain_ref, give_ref = refs[:-1]
        give_ref[:128, :] = grad_in.astype(BF16)
        give_ref[128:, :] = jnp.where(mine, gain_1[...], gain_row).astype(BF16)
        gain_ref[...] = jnp.where(mine, gain_row, gain_1[...])


def expert_grads_kernel(
    flag, acts_0, acts_1, sent_0, sent_1, up_hbm, down_hbm, held, made, sems, out_sems
):
    first = flag[0] == 1
    gets = {}
    for which in range(4):
        for e in range(2):
            part = pl.ds(384 * which + 192 * e, 192)
            gets[which, e] = [
                fetch(
                    first,
                    pair[0].at[part, :],
                    pair[1].at[part, :],
                    held.at[which, e, pl.ds(192 * side, 192), :],
                    sems.at[which, e, side],
                )
                for side, pair in enumerate(((acts_0, acts_1), (sent_0, sent_1)))
            ]
    puts = []
    for e in range(2):
        for index, (left, right, out) in enumerate(((0, 1, down_hbm), (2, 3, up_hbm))):
            for get in gets[left, e] + gets[right, e]:
                get.wait()
            made[2 * e + index] = tn(held[left, e], held[right, e])
            put = pltpu.make_async_copy(made.at[2 * e + index], out.at[e], out_sems.at[2 * e + index])
            put.start()
            puts.append(put)
    for put in puts:
        put.wait()


def gain_rows(gain):
    row = iota((8, 128), 0)
    out = jnp.zeros((8, 128), F32)
    for group in range(6):
        out = jnp.where(row == group, gain[:, 128 * group : 128 * (group + 1)], out)
    return out


def attend_grads_kernel(flag, acts_0, acts_1, sent_0, sent_1, packed_ref):
    first = flag[0] == 1
    own = picked(first, acts_0, acts_1)
    other = picked(first, sent_0, sent_1)

    def stacked(rows):
        return jnp.concatenate([own[rows], other[rows]], axis=0)

    left = stacked(slice(0, 128)).T.astype(BF16)
    packed_ref[:576, :768] = nn(left[:576], stacked(slice(128, 256)).astype(BF16)).astype(BF16)
    packed_ref[576:, :768] = nn(left[576:], stacked(slice(256, 384)).astype(BF16)).astype(BF16)
    small = (own[384:432] + other[384:432]).astype(BF16)
    for group in range(6):
        packed_ref[48 * group : 48 * (group + 1), 768:] = small[:, 128 * group : 128 * (group + 1)]
    packed_ref[288:, 768:] = jnp.zeros((480, 128), BF16)


def sum_shares_kernel(parts, gain, taken, out_ref):
    total = parts[0].astype(F32)
    for source in range(1, 16):
        total = total + parts[source].astype(F32)
    rows = gain_rows(gain[0:1] + taken[...].astype(F32)[128:129])
    side = jnp.concatenate([total[:40, 768:], rows], axis=0)
    share = jnp.concatenate([total[:, :768], side], axis=1).astype(BF16)
    for source in range(16):
        out_ref[source] = share


def unpack_kernel(shares, proj_ref, out_ref, router_ref, gain_a_ref, gain_m_ref, table_ref):
    whole = shares[...].astype(F32)
    for k in range(3):
        proj_ref[k] = whole[192 * k : 192 * (k + 1), :768]
    out_ref[...] = whole[576:, :768]
    gain = jnp.zeros((8, 128), F32)
    for block in range(16):
        gain = gain + whole[48 * block + 40 : 48 * block + 48, 768:]
    for group in range(6):
        lanes = slice(128 * group, 128 * (group + 1))
        router_ref[:, lanes] = whole[48 * group : 48 * group + 32, 768:]
        gain_m_ref[:, lanes] = whole[48 * group + 33 : 48 * group + 34, 768:]
        gain_a_ref[:, lanes] = gain[group : group + 1]
    table_ref[...] = whole[34:37, 768:800]


def prepare_kernel(flag, router, gain_a, gain_m, table, routes, small_ref, own_ref, give_ref):
    first = flag[0] == 1
    small_ref[:32, :] = router[...]
    row = iota((16, 768), 0)
    gains = jnp.where(row == 0, gain_a[...].astype(F32), jnp.where(row == 8, gain_m[...].astype(F32), 0.0))
    small_ref[32:48, :] = gains.astype(BF16)
    wide = jnp.concatenate([table[...].astype(F32), jnp.zeros((13, 32), F32)], axis=0)
    place = ones_where(iota((32, 768), 0) == iota((32, 768), 1)).astype(BF16)
    small_ref[48:64, :] = nn(wide.astype(BF16), place).astype(BF16)
    own_ref[...] = jnp.where(first, routes[0], routes[1])
    give_ref[...] = jnp.where(first, routes[1], routes[0])


def swap(array):
    return lax.ppermute(array, "section", [(0, 1), (1, 0)])


def to_second(array):
    return lax.ppermute(array, "section", [(0, 1)])


def to_first(array):
    return lax.ppermute(array, "section", [(1, 0)])


def ring(array, axis, by):
    size = lax.axis_size(axis)
    return lax.ppermute(array, axis, [(i, (i + by) % size) for i in range(size)])


def with_others(part):
    return (part, ring(part, "head", 2), ring(part, "head", 1), ring(part, "head", -1))


def exchange(rows):
    blocks = rows.reshape(16, rows.shape[0] // 16, rows.shape[1])
    return lax.all_to_all(blocks, "expert", 0, 0, tiled=True).reshape(rows.shape)


def sorting(stride, offsets):
    blocks = []
    for offset in offsets:
        for expert in range(2):
            at = np.arange(16)[:, None] * stride + offset + expert * 12 + np.arange(12)[None]
            blocks.append(at.reshape(-1))
    at = np.concatenate(blocks)
    table = np.zeros((at.size, 16 * stride), np.float32)
    table[np.arange(at.size), at] = 1.0
    return table.astype(ml_dtypes.bfloat16)


def on_device(
    inputs,
    cotangent,
    routes,
    attend_gain,
    query_key_value,
    attend_out,
    position_bias,
    mixture_gain,
    router,
    expert_up,
    expert_down,
):
    core = lax.axis_index("section")
    first = core == 0
    flags = [(core == which).astype(jnp.int32).reshape(1) for which in range(2)]
    small, route_own, route_give = call(
        prepare_kernel,
        "prepare",
        [((SMALL, 768), BF16), ((2, 128), jnp.int32), ((2, 128), jnp.int32)],
        [SMEM] + [VMEM] * 5,
        (
            flags[0],
            router[0].T,
            attend_gain,
            mixture_gain,
            position_bias[0],
            routes[0].transpose(0, 2, 1),
        ),
        limit=60,
    )
    small = (small, swap(small))
    w = query_key_value[0].transpose(0, 2, 1)
    w = (w, swap(w))
    o = (attend_out[0], swap(attend_out[0]))
    tiles = (route_own, swap(route_give))
    small_other, up, down = lax.optimization_barrier((small[1], expert_up[0], expert_down[0]))
    small = (small[0], small_other)
    up = (up, swap(up))
    down = (down, swap(down))

    row16 = ((128, 768), BF16)
    row32 = ((128, 768), F32)
    dma = pltpu.SemaphoreType.DMA
    attend_scratch = (pltpu.VMEM((3, 192, 768), BF16), pltpu.VMEM((192, 768), BF16), dma((2,)))

    def attend_forward(which, sources):
        return call(
            functools.partial(attend_forward_kernel, which == 1),
            f"attend{which}",
            [row16, row16, ((3, 128, 192), BF16), ((3, 128, 128), F32), ((128, 192), BF16), row16],
            [SMEM] + [VMEM] * (len(sources) + 2) + [ANY] * 4,
            (flags[which], *sources, *small, *w, *o),
            attend_scratch,
        )

    def dispatch(which, low, parts, extra):
        slots = 384 * (1 + which)
        mask = ((128, slots), BF16)
        return call(
            functools.partial(dispatch_kernel, which == 1),
            f"dispatch{which}",
            [row32, row16, ((128, 128), F32), mask, mask, mask, mask, ((slots, 768), BF16)]
            + [row16] * len(extra),
            [SMEM] + [VMEM] * (9 + len(extra)),
            (flags[which], low, *parts, *small, *tiles, *extra),
        )

    def expert_scratch(count):
        return (
            pltpu.VMEM((2, 768, 768), BF16),
            pltpu.VMEM((2, 768, 768), BF16),
            pltpu.VMEM((count, 768), BF16),
            dma((4,)),
        )

    def attend_backward(which, parts, gates, normed_m, middle, low, saved):
        return call(
            attend_backward_kernel,
            f"attend_back{which}",
            [row16, row32, ((432, 768), BF16)],
            [SMEM] + [VMEM] * 16 + [ANY] * 4,
            (flags[which], *parts, gates, *tiles, normed_m, middle, low, *small, *saved, *w, *o),
            attend_scratch,
        )

    low_0, normed_a0, heads_0, probs_0, mixed_0, part = attend_forward(
        0, (inputs,)
    )
    middle_0, normed_m0, gates_0, mix_0, rest_0, gap_0, take_0, buffer = dispatch(
        0, low_0, with_others(part), ()
    )
    sort_0, sort_1 = sorting(24, (0,)), sorting(48, (0, 24))
    unsort_0, unsort_1 = sort_0.T.copy(), sort_1.T.copy()
    block = ((384, 768), BF16)
    arrived, hidden, slope, rows = call(
        raise_kernel,
        "raise0",
        [block, block, block, block],
        [SMEM] + [VMEM] * 3 + [ANY] * 4,
        (flags[0], exchange(buffer), sort_0, unsort_0, *up, *down),
        expert_scratch(384),
    )
    part, gap_0 = call(
        combine_kernel, "combine0", [row16, row32], [VMEM] * 4, (exchange(rows), mix_0, rest_0, gap_0)
    )

    low_1, normed_a1, heads_1, probs_1, mixed_1, part = attend_forward(
        1, (middle_0, *with_others(part))
    )
    middle_1, normed_m1, gates_1, mix_1, rest_1, gap_1, take_1, buffer, cot = dispatch(
        1, low_1, with_others(part), (cotangent,)
    )
    acts_ffn1, rows = call(
        raise_lower_kernel,
        "raise_lower1",
        [((1536, 768), BF16), ((768, 768), BF16)],
        [SMEM] + [VMEM] * 3 + [ANY] * 4,
        (flags[1], exchange(buffer), sort_1, unsort_1, *up, *down),
        expert_scratch(768),
    )
    part, part_out = call(
        combine_both_kernel,
        "combine1",
        [((128, 896), BF16), row16],
        [VMEM] * 6,
        (exchange(rows), mix_1, rest_1, gap_1, take_1, cot),
    )
    part, grad_middle, acts_1 = attend_backward(
        1, with_others(part), gates_1, normed_m1, middle_1, cot, (normed_a1, heads_1, probs_1, mixed_1)
    )
    mask = [SMEM] + [VMEM] * 8
    gain = ((16, 768), F32)
    gain_1, grad_low, buffer, give, grad_1 = call(
        functools.partial(enter_kernel, True),
        "enter1",
        [gain, row16, block, row16, row32],
        mask + [VMEM] * 2,
        (flags[1], *with_others(part), grad_middle, low_1, *small, mix_0, rest_0),
    )
    taken_1 = swap(give)

    acts_ffn0, rows = call(
        lower_kernel,
        "lower0",
        [((1536, 768), BF16), block],
        [SMEM] + [VMEM] * 6 + [ANY] * 4,
        (flags[0], exchange(buffer), sort_0, unsort_0, arrived, hidden, slope, *up, *down),
        expert_scratch(384),
    )
    (part,) = call(
        combine_back_kernel,
        "combine_back0",
        [((128, 896), BF16)],
        [VMEM] * 4,
        (exchange(rows), take_0, gap_0, grad_low),
    )
    part, grad_middle, acts_0 = attend_backward(
        0, with_others(part), gates_0, normed_m0, middle_0, grad_low, (normed_a0, heads_0, probs_0, mixed_0)
    )
    (packed,) = call(
        attend_grads_kernel,
        "attend_grads",
        [((768, 896), BF16)],
        [SMEM] + [VMEM] * 4,
        (flags[0], acts_0, acts_1, to_first(acts_0), to_second(acts_1)),
    )
    packed, acts_ffn0, acts_ffn1 = lax.optimization_barrier((packed, acts_ffn0, acts_ffn1))
    shares = exchange(packed)
    gain_mine, give, grad_0 = call(
        functools.partial(enter_kernel, False),
        "enter0",
        [gain, ((144, 768), BF16), row32],
        mask + [VMEM],
        (flags[0], *with_others(part), grad_middle, low_0, *small, gain_1),
    )
    taken_0 = swap(give)
    grad_up, grad_down = call(
        expert_grads_kernel,
        "expert_grads",
        [((2, 768, 768), F32), ((2, 768, 768), F32)],
        [SMEM] + [ANY] * 4,
        (flags[0], acts_ffn0, acts_ffn1, to_first(acts_ffn0), to_second(acts_ffn1)),
        (
            pltpu.VMEM((4, 2, 384, 768), BF16),
            pltpu.VMEM((4, 768, 768), F32),
            dma((4, 2, 2)),
            dma((4,)),
        ),
        [ANY] * 2,
        flops=4 * 10**9,
        size=20 * 2**20,
    )
    (shares,) = call(
        sum_shares_kernel,
        "sum_shares",
        [((16, 48, 896), BF16)],
        [VMEM] * 3,
        (shares.reshape(16, 48, 896), gain_mine, taken_0),
    )
    taken_0, part_out = lax.optimization_barrier((taken_0, part_out))
    out_1 = (middle_1 + summed(with_others(part_out))).astype(BF16)
    grad_proj, grad_out, grad_router, grad_gain_a, grad_gain_m, grad_table = call(
        unpack_kernel,
        "unpack",
        [
            ((3, 192, 768), F32),
            ((192, 768), F32),
            ((32, 768), F32),
            ((1, 768), F32),
            ((1, 768), F32),
            ((3, 32), F32),
        ],
        [VMEM],
        (exchange(shares.reshape(768, 896)),),
    )
    taken_0 = taken_0[:128]
    section_output = jnp.stack(
        [jnp.where(first, low_1, to_second(out_1)), jnp.where(first, taken_1, out_1)]
    )
    input_grad = jnp.stack(
        [
            jnp.where(first, grad_0, taken_1.astype(F32)),
            jnp.where(first, taken_0.astype(F32), grad_1),
        ]
    )
    return (
        section_output[None],
        input_grad[None],
        grad_gain_a,
        grad_proj.transpose(0, 2, 1)[None],
        grad_out[None],
        grad_table[None],
        grad_gain_m,
        grad_router.T[None],
        grad_up[None],
        grad_down[None],
    )


def solution(mesh):
    return jax.shard_map(
        on_device,
        mesh=mesh,
        in_specs=(
            P(None, "expert", None),
            P(None, "expert", None),
            P("section", None, "expert", None),
            P("section", None),
            P("section", None, None, "head"),
            P("section", "head", None),
            P("section", "head", None),
            P("section", None),
            P("section", None, None),
            P("section", "expert", None, "head"),
            P("section", "expert", "head", None),
        ),
        out_specs=(
            P("section", None, "expert", None),
            P("section", None, "expert", None),
            P("section", None),
            P("section", None, None, "head"),
            P("section", "head", None),
            P("section", "head", None),
            P("section", None),
            P("section", None, None),
            P("section", "expert", None, "head"),
            P("section", "expert", "head", None),
        ),
        check_vma=False,
    )
```

```python
import functools

import jax
import jax.numpy as jnp
import ml_dtypes
import numpy as np
from jax import lax
from jax.experimental import pallas as pl
from jax.experimental.pallas import tpu as pltpu
from jax.sharding import PartitionSpec as P

HEAD_DIM = 64
EPS = 1e-06
NEG = -1e30
F32 = jnp.float32
BF16 = jnp.bfloat16
GAIN_A, GAIN_M, TABLE, SMALL = 32, 40, 48, 64

VMEM = pl.BlockSpec(memory_space=pltpu.VMEM)
SMEM = pl.BlockSpec(memory_space=pltpu.SMEM)
ANY = pl.BlockSpec(memory_space=pl.ANY)


def call(kernel, name, out_shape, in_specs, args, scratch=(), out_specs=None, flops=10**9, size=2**20, limit=48):
    return pl.pallas_call(
        kernel,
        name=name,
        out_shape=[jax.ShapeDtypeStruct(shape, dtype) for shape, dtype in out_shape],
        in_specs=in_specs,
        out_specs=out_specs or [VMEM] * len(out_shape),
        scratch_shapes=list(scratch),
        compiler_params=pltpu.CompilerParams(vmem_limit_bytes=limit * 2**20),
        cost_estimate=pl.CostEstimate(flops=flops, bytes_accessed=size, transcendentals=0),
    )(*args)


def nn(a, b):
    return lax.dot_general(a, b, (((1,), (0,)), ((), ())), preferred_element_type=F32)


def nt(a, b):
    return lax.dot_general(a, b, (((1,), (1,)), ((), ())), preferred_element_type=F32)


def tn(a, b):
    return lax.dot_general(a, b, (((0,), (0,)), ((), ())), preferred_element_type=F32)


def iota(shape, dim):
    return lax.broadcasted_iota(jnp.int32, shape, dim)


def ones_where(mask):
    return jnp.where(mask, 1.0, 0.0)


def flipped(array):
    return array.astype(F32).T.astype(BF16)


def norm_scale(values):
    return lax.rsqrt(jnp.mean(values * values, axis=-1, keepdims=True) + EPS)


def norm_back(grad_normed, values, scale, gain):
    unit = values * scale
    grad_gain = jnp.sum(grad_normed * unit, axis=0, keepdims=True)
    grad_unit = grad_normed * gain
    grad_values = scale * (grad_unit - unit * jnp.mean(grad_unit * unit, axis=-1, keepdims=True))
    return (grad_values, grad_gain)


def summed(parts):
    own, far, left, right = [part[...].astype(F32) for part in parts]
    return (own + far) + (left + right)


def fetch(mine, own, other, out, sem):
    @pl.when(mine)
    def _():
        pltpu.make_async_copy(own, out, sem).start()

    @pl.when(jnp.logical_not(mine))
    def _():
        pltpu.make_async_copy(other, out, sem).start()

    return pltpu.make_async_copy(own, out, sem)


def picked(mine, own, other):
    return jnp.where(mine, own[...].astype(F32), other[...].astype(F32))


def route_columns(mine, own, other):
    rows = jnp.where(mine, own[...], other[...])
    eye = iota((128, 128), 0) == iota((128, 128), 1)
    return [jnp.sum(jnp.where(eye, rows[k : k + 1], 0), axis=-1, keepdims=True) for k in range(2)]


def bucket_of_lane():
    offset = (128 - iota((128, 128), 1)) & 127
    return ones_where(jnp.minimum(offset, 31) == iota((128, 128), 0)).astype(BF16)


def head_mask(head):
    lane = iota((128, 3 * HEAD_DIM), 1)
    return (lane >= head * HEAD_DIM) & (lane < (head + 1) * HEAD_DIM)


def gelu_both(pre):
    inner = 0.7978845608028654
    cube = 0.044715
    square = pre * pre
    slope = jnp.tanh(inner * pre * (1.0 + cube * square))
    half = 0.5 * (1.0 + slope)
    value = pre * half
    grad = half + 0.5 * pre * (1.0 - slope * slope) * inner * (1.0 + 3.0 * cube * square)
    return (value, grad)


def attend_forward_kernel(
    chained,
    flag,
    *refs,
):
    mine = flag[0] == 1
    if chained:
        middle, own, far, left, right = refs[:5]
        refs = refs[5:]
    else:
        source = refs[0]
        refs = refs[1:]
    small_own, small_other, w_own, w_other, o_own, o_other = refs[:6]
    low, normed_ref, heads_ref, probs_ref, mixed_ref, part_ref = refs[6:12]
    w, o, sems = refs[12:]
    get_w = fetch(mine, w_own, w_other, w, sems.at[0])
    get_o = fetch(mine, o_own, o_other, o, sems.at[1])
    if chained:
        low[...] = (middle[...] + summed((own, far, left, right))).astype(BF16)
    else:
        low[...] = picked(mine, source.at[0], source.at[1]).astype(BF16)
    values = low[...].astype(F32)
    small = picked(mine, small_own, small_other)
    normed = (values * norm_scale(values) * small[GAIN_A : GAIN_A + 1]).astype(BF16)
    normed_ref[...] = normed
    table = small[TABLE : TABLE + 8, :128].astype(BF16)
    levels = nn(table, bucket_of_lane())
    causal = iota((128, 128), 0) >= iota((128, 128), 1)
    get_w.wait()
    query, key, value = [nt(normed, w[k]) for k in range(3)]
    key, value = key.astype(BF16), value.astype(BF16)
    heads_ref[0] = query.astype(BF16)
    heads_ref[1] = key
    heads_ref[2] = value
    query = heads_ref[0].astype(F32)
    mixed = jnp.zeros((128, 3 * HEAD_DIM), F32)
    for head in range(3):
        mask = head_mask(head)
        bias = pltpu.roll(
            jnp.broadcast_to(levels[head : head + 1], (128, 128)), 0, 1, stride=1, stride_axis=0
        )
        scores = nt(jnp.where(mask, query, 0.0).astype(BF16), key) * HEAD_DIM ** (-0.5) + bias
        scores = jnp.where(causal, scores, NEG)
        weights = jnp.exp(scores - jnp.max(scores, axis=-1, keepdims=True))
        probs = weights / jnp.sum(weights, axis=-1, keepdims=True)
        probs_ref[head] = probs
        mixed = jnp.where(mask, nn(probs.astype(BF16), value), mixed)
    mixed_ref[...] = mixed.astype(BF16)
    get_o.wait()
    part_ref[...] = nn(mixed_ref[...], o[...]).astype(BF16)


def dispatch_kernel(
    both,
    flag,
    low,
    own,
    far,
    left,
    right,
    small_own,
    small_other,
    route_own,
    route_other,
    *refs,
):
    if both:
        cotangents, cotangent = refs[0], refs[-1]
        cotangent[...] = picked(flag[0] == 0, cotangents.at[0], cotangents.at[1]).astype(BF16)
        refs = refs[1:-1]
    middle_ref, normed_ref, gates_ref, mix_ref, rest_ref, gap_ref, take_ref, buffer_ref = refs[:8]
    mine = flag[0] == 1
    middle = low[...].astype(F32) + summed((own, far, left, right))
    middle_ref[...] = middle
    small = picked(mine, small_own, small_other)
    normed = (middle * norm_scale(middle) * small[GAIN_M : GAIN_M + 1]).astype(BF16)
    normed_ref[...] = normed
    logits = nt(normed, small[:32].astype(BF16))
    lane = iota((128, 32), 1)
    route = route_columns(mine, route_own, route_other)
    pick = [ones_where(one == lane) for one in route]
    before = nn(
        ones_where(iota((128, 128), 1) < iota((128, 128), 0)).astype(BF16),
        (pick[0] + pick[1]).astype(BF16),
    )
    chosen = [jnp.sum(logits * one, axis=-1, keepdims=True) for one in pick]
    top = jnp.maximum(chosen[0], chosen[1])
    weights = [jnp.exp(one - top) for one in chosen]
    total = weights[0] + weights[1]
    gates = [one / total for one in weights]
    wide = iota((128, 128), 1)
    gates_ref[...] = jnp.where(wide == 0, gates[0], jnp.where(wide == 1, gates[1], 0.0))
    place = [jnp.sum(before * one, axis=-1, keepdims=True).astype(jnp.int32) for one in pick]
    stride = 48 if both else 24
    slots = 16 * stride
    target = [(e >> 1) * stride + (e & 1) * 12 + at for e, at in zip(route, place)]
    slot = iota((128, slots), 1)
    mask = [ones_where(slot == one) for one in target]
    spread = mask[0] + mask[1]
    weighted = mask[0] * gates[0] + mask[1] * gates[1]
    high = weighted.astype(BF16)
    mix_ref[...] = high
    rest_ref[...] = (weighted - high.astype(F32)).astype(BF16)
    gap_ref[...] = (mask[0] - mask[1]).astype(BF16)
    buffer = nn(spread.T.astype(BF16), normed)
    if both:
        mask = [ones_where(slot == one + 24) for one in target]
        take_ref[...] = (mask[0] + mask[1]).astype(BF16)
        weighted = (mask[0] * gates[0] + mask[1] * gates[1]).T
        high = weighted.astype(BF16)
        rest = (weighted - high.astype(F32)).astype(BF16)
        buffer = buffer + (nn(high, cotangent[...]) + nn(rest, cotangent[...]))
    else:
        take_ref[...] = spread.astype(BF16)
    buffer_ref[...] = buffer.astype(BF16)


def raise_kernel(
    flag,
    raw,
    sort,
    unsort,
    up_own,
    up_other,
    down_own,
    down_other,
    arrived_ref,
    hidden_ref,
    slope_ref,
    rows_ref,
    up,
    down,
    rows,
    sems,
):
    mine = flag[0] == 1
    gets = [fetch(mine, up_own.at[e], up_other.at[e], up.at[e], sems.at[e]) for e in range(2)]
    gets += [fetch(mine, down_own.at[e], down_other.at[e], down.at[e], sems.at[2 + e]) for e in range(2)]
    arrived_ref[...] = nn(sort[...], raw[...]).astype(BF16)
    for e in range(2):
        part = pl.ds(192 * e, 192)
        gets[e].wait()
        value, slope = gelu_both(nn(arrived_ref[part, :], up[e]))
        hidden_ref[part, :] = value.astype(BF16)
        slope_ref[part, :] = slope.astype(BF16)
        gets[2 + e].wait()
        rows[part, :] = nn(hidden_ref[part, :], down[e]).astype(BF16)
    rows_ref[...] = nn(unsort[...], rows[...]).astype(BF16)


def lower_kernel(
    flag,
    raw,
    sort,
    unsort,
    arrived,
    hidden,
    slope,
    up_own,
    up_other,
    down_own,
    down_other,
    acts_ref,
    rows_ref,
    up,
    down,
    rows,
    sems,
):
    mine = flag[0] == 1
    gets = [fetch(mine, down_own.at[e], down_other.at[e], down.at[e], sems.at[2 + e]) for e in range(2)]
    gets += [fetch(mine, up_own.at[e], up_other.at[e], up.at[e], sems.at[e]) for e in range(2)]
    acts_ref[0:384, :] = hidden[...]
    acts_ref[768:1152, :] = arrived[...]
    acts_ref[384:768, :] = nn(sort[...], raw[...]).astype(BF16)
    for e in range(2):
        part = pl.ds(192 * e, 192)
        gets[e].wait()
        grad_hidden = nt(acts_ref[pl.ds(384 + 192 * e, 192), :], down[e])
        acts_ref[pl.ds(1152 + 192 * e, 192), :] = (slope[part, :].astype(F32) * grad_hidden).astype(BF16)
        gets[2 + e].wait()
        rows[part, :] = nt(acts_ref[pl.ds(1152 + 192 * e, 192), :], up[e]).astype(BF16)
    rows_ref[...] = nn(unsort[...], rows[...]).astype(BF16)


def raise_lower_kernel(
    flag,
    raw,
    sort,
    unsort,
    up_own,
    up_other,
    down_own,
    down_other,
    acts_ref,
    rows_ref,
    up,
    down,
    rows,
    sems,
):
    mine = flag[0] == 1
    gets = [fetch(mine, up_own.at[e], up_other.at[e], up.at[e], sems.at[e]) for e in range(2)]
    gets += [fetch(mine, down_own.at[e], down_other.at[e], down.at[e], sems.at[2 + e]) for e in range(2)]
    both = nn(sort[...], raw[...]).astype(BF16)
    acts_ref[768:1152, :] = both[:384]
    acts_ref[384:768, :] = both[384:]
    for e in range(2):
        part = pl.ds(192 * e, 192)
        behind = pl.ds(384 + 192 * e, 192)
        gets[e].wait()
        value, slope = gelu_both(nn(acts_ref[pl.ds(768 + 192 * e, 192), :], up[e]))
        acts_ref[part, :] = value.astype(BF16)
        gets[2 + e].wait()
        rows[part, :] = nn(acts_ref[part, :], down[e]).astype(BF16)
        grad_hidden = nt(acts_ref[pl.ds(384 + 192 * e, 192), :], down[e])
        acts_ref[pl.ds(1152 + 192 * e, 192), :] = (slope * grad_hidden).astype(BF16)
        rows[behind, :] = nt(acts_ref[pl.ds(1152 + 192 * e, 192), :], up[e]).astype(BF16)
    rows_ref[...] = nn(unsort[...], rows[...]).astype(BF16)


def combine_kernel(returned, mix, rest, gap, part_ref, gap_ref):
    rows = returned[...]
    part_ref[...] = (nn(mix[...], rows) + nn(rest[...], rows)).astype(BF16)
    gap_ref[...] = nn(gap[...], rows)


def side_columns(difference):
    lane = iota((128, 128), 1)
    high = difference.astype(BF16).astype(F32)
    return jnp.where(lane == 0, high, jnp.where(lane == 1, difference - high, 0.0)).astype(BF16)


def combine_back_kernel(returned, take, gap, low, part_ref):
    part_ref[:, :768] = nn(take[...], returned[...]).astype(BF16)
    difference = jnp.sum(low[...].astype(F32) * gap[...], axis=-1, keepdims=True)
    part_ref[:, 768:] = side_columns(difference)


def combine_both_kernel(returned, mix, rest, gap, take, low, part_ref, out_ref):
    rows = returned[...]
    part_ref[:, :768] = nn(take[...], rows).astype(BF16)
    difference = jnp.sum(low[...].astype(F32) * nn(gap[...], rows), axis=-1, keepdims=True)
    part_ref[:, 768:] = side_columns(difference)
    out_ref[...] = (nn(mix[...], rows) + nn(rest[...], rows)).astype(BF16)


def attend_backward_kernel(
    flag,
    own,
    far,
    left,
    right,
    gates,
    route_own,
    route_other,
    normed_m,
    middle,
    low,
    small_own,
    small_other,
    normed_a,
    heads,
    probs,
    mixed,
    w_own,
    w_other,
    o_own,
    o_other,
    *refs,
):
    part_ref, middle_ref, acts_ref, w, o, sems = refs
    mine = flag[0] == 1
    get_o = fetch(mine, o_own, o_other, o, sems.at[1])
    get_w = fetch(mine, w_own, w_other, w, sems.at[0])
    total = summed((own, far, left, right))
    small = picked(mine, small_own, small_other)
    grad_normed = total[:, :768]
    difference = total[:, 768:769] + total[:, 769:770]
    grad_first = gates[:, 0:1] * gates[:, 1:2] * difference
    lane = iota((128, 128), 1)
    route = route_columns(mine, route_own, route_other)
    sign = ones_where(route[0] == lane) - ones_where(route[1] == lane)
    grad_logits = (grad_first * sign).astype(BF16).astype(F32)
    grad_router = nn(grad_logits.T.astype(BF16), normed_m[...])
    grad_normed = grad_normed + nn(grad_logits[:, :32].astype(BF16), small[:32].astype(BF16))
    grad_out = low[...].astype(F32)
    values = middle[...]
    grad_values, grad_gain = norm_back(
        grad_normed, values, norm_scale(values), small[GAIN_M : GAIN_M + 1]
    )
    grad_middle = grad_out + grad_values
    middle_ref[...] = grad_middle
    grad_attn = grad_middle.astype(BF16)
    acts_ref[128:256, :] = normed_a[...]
    acts_ref[256:384, :] = grad_attn
    get_o.wait()
    grad_mixed = nt(grad_attn, o[...]).astype(BF16)
    wide_mixed = grad_mixed.astype(F32)
    query, key, value = heads[0], heads[1], heads[2]
    zero = jnp.zeros((128, 3 * HEAD_DIM), F32)
    grads = [zero, zero, zero]
    turned = ones_where(iota((128, 128), 0) + iota((128, 128), 1) == 127).astype(BF16)
    levels = bucket_of_lane()
    tables = []
    for head in range(3):
        mask = head_mask(head)
        p = probs[head]
        grad_probs = nt(jnp.where(mask, wide_mixed, 0.0).astype(BF16), value)
        delta = jnp.sum(p * grad_probs, axis=-1, keepdims=True)
        grad_scores = (p * (grad_probs - delta)).astype(BF16)
        grads[0] = jnp.where(mask, nn(grad_scores, key), grads[0])
        grads[1] = jnp.where(mask, nn(flipped(grad_scores), query), grads[1])
        grads[2] = jnp.where(mask, nn(p.T.astype(BF16), grad_mixed), grads[2])
        skewed = pltpu.roll(nn(turned, grad_scores), 1, 1, stride=1, stride_axis=0)
        tables.append(jnp.sum(skewed, axis=0, keepdims=True))
    factor = HEAD_DIM ** (-0.5)
    grads = [(grads[0] * factor).astype(BF16), (grads[1] * factor).astype(BF16), grads[2].astype(BF16)]
    get_w.wait()
    part_ref[:128, :] = (nn(grads[0], w[0]) + nn(grads[1], w[1]) + nn(grads[2], w[2])).astype(BF16)
    placed = jnp.zeros((128, 768), F32)
    away = iota((192, 768), 1) - iota((192, 768), 0)
    for k, one in enumerate(grads + [mixed[...]]):
        placed = placed + nn(one, ones_where(away == 192 * k).astype(BF16))
    acts_ref[:128, :] = placed.astype(BF16)
    row = iota((8, 128), 0)
    stacked = jnp.zeros((8, 128), F32)
    for head in range(3):
        stacked = jnp.where(row == 2 + head, tables[head], stacked)
    level_sums = lax.dot_general(
        stacked,
        levels.astype(F32),
        (((1,), (1,)), ((), ())),
        precision=lax.Precision.HIGHEST,
        preferred_element_type=F32,
    )
    row = iota((16, 768), 0)
    last = jnp.concatenate([level_sums, jnp.zeros((8, 640), F32)], axis=1)
    last = jnp.concatenate([last, jnp.zeros((8, 768), F32)], axis=0)
    last = jnp.where(row == 1, grad_gain, last)
    acts_ref[384:432, :] = jnp.concatenate([grad_router[:32], last], axis=0).astype(BF16)


def enter_kernel(chained, flag, own, far, left, right, grad_middle, low, small_own, small_other, *refs):
    mine = flag[0] == 1
    small = picked(mine, small_own, small_other)
    values = low[...].astype(F32)
    total = summed((own, far, left, right))
    grad_values, grad_gain = norm_back(
        total, values, norm_scale(values), small[GAIN_A : GAIN_A + 1]
    )
    grad_in = grad_values + grad_middle[...]
    grad_ref = refs[-1]
    grad_ref[...] = grad_in
    gain_row = jnp.broadcast_to(grad_gain, (16, 768))
    if chained:
        mix, rest, gain_ref, low_ref, buffer_ref, give_ref = refs[:-1]
        grad_low = grad_in.astype(BF16)
        low_ref[...] = grad_low
        buffer = nn(flipped(mix[...]), grad_low) + nn(flipped(rest[...]), grad_low)
        buffer_ref[...] = buffer.astype(BF16)
        gain_ref[...] = gain_row
        give_ref[...] = picked(mine, low, low_ref).astype(BF16)
    else:
        gain_1, gain_ref, give_ref = refs[:-1]
        give_ref[:128, :] = grad_in.astype(BF16)
        give_ref[128:, :] = jnp.where(mine, gain_1[...], gain_row).astype(BF16)
        gain_ref[...] = jnp.where(mine, gain_row, gain_1[...])


def expert_grads_kernel(
    flag, acts_0, acts_1, sent_0, sent_1, up_hbm, down_hbm, held, made, sems, out_sems
):
    first = flag[0] == 1
    gets = {}
    for which in range(4):
        for e in range(2):
            part = pl.ds(384 * which + 192 * e, 192)
            gets[which, e] = [
                fetch(
                    first,
                    pair[0].at[part, :],
                    pair[1].at[part, :],
                    held.at[which, e, pl.ds(192 * side, 192), :],
                    sems.at[which, e, side],
                )
                for side, pair in enumerate(((acts_0, acts_1), (sent_0, sent_1)))
            ]
    puts = []
    for e in range(2):
        for index, (left, right, out) in enumerate(((0, 1, down_hbm), (2, 3, up_hbm))):
            for get in gets[left, e] + gets[right, e]:
                get.wait()
            made[2 * e + index] = tn(held[left, e], held[right, e])
            put = pltpu.make_async_copy(made.at[2 * e + index], out.at[e], out_sems.at[2 * e + index])
            put.start()
            puts.append(put)
    for put in puts:
        put.wait()


def gain_rows(gain):
    row = iota((8, 128), 0)
    out = jnp.zeros((8, 128), F32)
    for group in range(6):
        out = jnp.where(row == group, gain[:, 128 * group : 128 * (group + 1)], out)
    return out


def attend_grads_kernel(flag, acts_0, acts_1, sent_0, sent_1, packed_ref):
    first = flag[0] == 1
    own = picked(first, acts_0, acts_1)
    other = picked(first, sent_0, sent_1)

    def stacked(rows):
        return jnp.concatenate([own[rows], other[rows]], axis=0)

    left = stacked(slice(0, 128)).T.astype(BF16)
    packed_ref[:576, :768] = nn(left[:576], stacked(slice(128, 256)).astype(BF16)).astype(BF16)
    packed_ref[576:, :768] = nn(left[576:], stacked(slice(256, 384)).astype(BF16)).astype(BF16)
    small = (own[384:432] + other[384:432]).astype(BF16)
    for group in range(6):
        packed_ref[48 * group : 48 * (group + 1), 768:] = small[:, 128 * group : 128 * (group + 1)]
    packed_ref[288:, 768:] = jnp.zeros((480, 128), BF16)


def sum_shares_kernel(parts, gain, taken, out_ref):
    total = parts[0].astype(F32)
    for source in range(1, 16):
        total = total + parts[source].astype(F32)
    rows = gain_rows(gain[0:1] + taken[...].astype(F32)[128:129])
    side = jnp.concatenate([total[:40, 768:], rows], axis=0)
    share = jnp.concatenate([total[:, :768], side], axis=1).astype(BF16)
    for source in range(16):
        out_ref[source] = share


def unpack_kernel(shares, proj_ref, out_ref, router_ref, gain_a_ref, gain_m_ref, table_ref):
    whole = shares[...].astype(F32)
    for k in range(3):
        proj_ref[k] = whole[192 * k : 192 * (k + 1), :768]
    out_ref[...] = whole[576:, :768]
    gain = jnp.zeros((8, 128), F32)
    for block in range(16):
        gain = gain + whole[48 * block + 40 : 48 * block + 48, 768:]
    for group in range(6):
        lanes = slice(128 * group, 128 * (group + 1))
        router_ref[:, lanes] = whole[48 * group : 48 * group + 32, 768:]
        gain_m_ref[:, lanes] = whole[48 * group + 33 : 48 * group + 34, 768:]
        gain_a_ref[:, lanes] = gain[group : group + 1]
    table_ref[...] = whole[34:37, 768:800]


def prepare_kernel(flag, router, gain_a, gain_m, table, routes, small_ref, own_ref, give_ref):
    first = flag[0] == 1
    small_ref[:32, :] = router[...]
    row = iota((16, 768), 0)
    gains = jnp.where(row == 0, gain_a[...].astype(F32), jnp.where(row == 8, gain_m[...].astype(F32), 0.0))
    small_ref[32:48, :] = gains.astype(BF16)
    wide = jnp.concatenate([table[...].astype(F32), jnp.zeros((13, 32), F32)], axis=0)
    place = ones_where(iota((32, 768), 0) == iota((32, 768), 1)).astype(BF16)
    small_ref[48:64, :] = nn(wide.astype(BF16), place).astype(BF16)
    own_ref[...] = jnp.where(first, routes[0], routes[1])
    give_ref[...] = jnp.where(first, routes[1], routes[0])


def swap(array):
    return lax.ppermute(array, "section", [(0, 1), (1, 0)])


def to_second(array):
    return lax.ppermute(array, "section", [(0, 1)])


def to_first(array):
    return lax.ppermute(array, "section", [(1, 0)])


def ring(array, axis, by):
    size = lax.axis_size(axis)
    return lax.ppermute(array, axis, [(i, (i + by) % size) for i in range(size)])


def with_others(part):
    return (part, ring(part, "head", 2), ring(part, "head", 1), ring(part, "head", -1))


def exchange(rows):
    blocks = rows.reshape(16, rows.shape[0] // 16, rows.shape[1])
    return lax.all_to_all(blocks, "expert", 0, 0, tiled=True).reshape(rows.shape)


def sorting(stride, offsets):
    blocks = []
    for offset in offsets:
        for expert in range(2):
            at = np.arange(16)[:, None] * stride + offset + expert * 12 + np.arange(12)[None]
            blocks.append(at.reshape(-1))
    at = np.concatenate(blocks)
    table = np.zeros((at.size, 16 * stride), np.float32)
    table[np.arange(at.size), at] = 1.0
    return table.astype(ml_dtypes.bfloat16)


def on_device(
    inputs,
    cotangent,
    routes,
    attend_gain,
    query_key_value,
    attend_out,
    position_bias,
    mixture_gain,
    router,
    expert_up,
    expert_down,
):
    core = lax.axis_index("section")
    first = core == 0
    flags = [(core == which).astype(jnp.int32).reshape(1) for which in range(2)]
    small, route_own, route_give = call(
        prepare_kernel,
        "prepare",
        [((SMALL, 768), BF16), ((2, 128), jnp.int32), ((2, 128), jnp.int32)],
        [SMEM] + [VMEM] * 5,
        (
            flags[0],
            router[0].T,
            attend_gain,
            mixture_gain,
            position_bias[0],
            routes[0].transpose(0, 2, 1),
        ),
        limit=60,
    )
    small = (small, swap(small))
    w = query_key_value[0].transpose(0, 2, 1)
    w = (w, swap(w))
    o = (attend_out[0], swap(attend_out[0]))
    tiles = (route_own, swap(route_give))
    small_other, w_other, o_other, up, down = lax.optimization_barrier(
        (small[1], w[1], o[1], expert_up[0], expert_down[0])
    )
    small, w, o = (small[0], small_other), (w[0], w_other), (o[0], o_other)
    up = (up, swap(up))
    down = (down, swap(down))

    row16 = ((128, 768), BF16)
    row32 = ((128, 768), F32)
    dma = pltpu.SemaphoreType.DMA
    attend_scratch = (pltpu.VMEM((3, 192, 768), BF16), pltpu.VMEM((192, 768), BF16), dma((2,)))

    def attend_forward(which, sources):
        return call(
            functools.partial(attend_forward_kernel, which == 1),
            f"attend{which}",
            [row16, row16, ((3, 128, 192), BF16), ((3, 128, 128), F32), ((128, 192), BF16), row16],
            [SMEM] + [VMEM] * (len(sources) + 2) + [ANY] * 4,
            (flags[which], *sources, *small, *w, *o),
            attend_scratch,
        )

    def dispatch(which, low, parts, extra):
        slots = 384 * (1 + which)
        mask = ((128, slots), BF16)
        return call(
            functools.partial(dispatch_kernel, which == 1),
            f"dispatch{which}",
            [row32, row16, ((128, 128), F32), mask, mask, mask, mask, ((slots, 768), BF16)]
            + [row16] * len(extra),
            [SMEM] + [VMEM] * (9 + len(extra)),
            (flags[which], low, *parts, *small, *tiles, *extra),
        )

    def expert_scratch(count):
        return (
            pltpu.VMEM((2, 768, 768), BF16),
            pltpu.VMEM((2, 768, 768), BF16),
            pltpu.VMEM((count, 768), BF16),
            dma((4,)),
        )

    def attend_backward(which, parts, gates, normed_m, middle, low, saved):
        return call(
            attend_backward_kernel,
            f"attend_back{which}",
            [row16, row32, ((432, 768), BF16)],
            [SMEM] + [VMEM] * 16 + [ANY] * 4,
            (flags[which], *parts, gates, *tiles, normed_m, middle, low, *small, *saved, *w, *o),
            attend_scratch,
        )

    low_0, normed_a0, heads_0, probs_0, mixed_0, part = attend_forward(
        0, (inputs,)
    )
    middle_0, normed_m0, gates_0, mix_0, rest_0, gap_0, take_0, buffer = dispatch(
        0, low_0, with_others(part), ()
    )
    sort_0, sort_1 = sorting(24, (0,)), sorting(48, (0, 24))
    unsort_0, unsort_1 = sort_0.T.copy(), sort_1.T.copy()
    block = ((384, 768), BF16)
    arrived, hidden, slope, rows = call(
        raise_kernel,
        "raise0",
        [block, block, block, block],
        [SMEM] + [VMEM] * 3 + [ANY] * 4,
        (flags[0], exchange(buffer), sort_0, unsort_0, *up, *down),
        expert_scratch(384),
    )
    part, gap_0 = call(
        combine_kernel, "combine0", [row16, row32], [VMEM] * 4, (exchange(rows), mix_0, rest_0, gap_0)
    )

    low_1, normed_a1, heads_1, probs_1, mixed_1, part = attend_forward(
        1, (middle_0, *with_others(part))
    )
    middle_1, normed_m1, gates_1, mix_1, rest_1, gap_1, take_1, buffer, cot = dispatch(
        1, low_1, with_others(part), (cotangent,)
    )
    acts_ffn1, rows = call(
        raise_lower_kernel,
        "raise_lower1",
        [((1536, 768), BF16), ((768, 768), BF16)],
        [SMEM] + [VMEM] * 3 + [ANY] * 4,
        (flags[1], exchange(buffer), sort_1, unsort_1, *up, *down),
        expert_scratch(768),
    )
    part, part_out = call(
        combine_both_kernel,
        "combine1",
        [((128, 896), BF16), row16],
        [VMEM] * 6,
        (exchange(rows), mix_1, rest_1, gap_1, take_1, cot),
    )
    part, grad_middle, acts_1 = attend_backward(
        1, with_others(part), gates_1, normed_m1, middle_1, cot, (normed_a1, heads_1, probs_1, mixed_1)
    )
    mask = [SMEM] + [VMEM] * 8
    gain = ((16, 768), F32)
    gain_1, grad_low, buffer, give, grad_1 = call(
        functools.partial(enter_kernel, True),
        "enter1",
        [gain, row16, block, row16, row32],
        mask + [VMEM] * 2,
        (flags[1], *with_others(part), grad_middle, low_1, *small, mix_0, rest_0),
    )
    taken_1 = swap(give)

    acts_ffn0, rows = call(
        lower_kernel,
        "lower0",
        [((1536, 768), BF16), block],
        [SMEM] + [VMEM] * 6 + [ANY] * 4,
        (flags[0], exchange(buffer), sort_0, unsort_0, arrived, hidden, slope, *up, *down),
        expert_scratch(384),
    )
    (part,) = call(
        combine_back_kernel,
        "combine_back0",
        [((128, 896), BF16)],
        [VMEM] * 4,
        (exchange(rows), take_0, gap_0, grad_low),
    )
    part, grad_middle, acts_0 = attend_backward(
        0, with_others(part), gates_0, normed_m0, middle_0, grad_low, (normed_a0, heads_0, probs_0, mixed_0)
    )
    (packed,) = call(
        attend_grads_kernel,
        "attend_grads",
        [((768, 896), BF16)],
        [SMEM] + [VMEM] * 4,
        (flags[0], acts_0, acts_1, to_first(acts_0), to_second(acts_1)),
    )
    packed, acts_ffn0, acts_ffn1 = lax.optimization_barrier((packed, acts_ffn0, acts_ffn1))
    shares = exchange(packed)
    gain_mine, give, grad_0 = call(
        functools.partial(enter_kernel, False),
        "enter0",
        [gain, ((144, 768), BF16), row32],
        mask + [VMEM],
        (flags[0], *with_others(part), grad_middle, low_0, *small, gain_1),
    )
    taken_0 = swap(give)
    grad_up, grad_down = call(
        expert_grads_kernel,
        "expert_grads",
        [((2, 768, 768), F32), ((2, 768, 768), F32)],
        [SMEM] + [ANY] * 4,
        (flags[0], acts_ffn0, acts_ffn1, to_first(acts_ffn0), to_second(acts_ffn1)),
        (
            pltpu.VMEM((4, 2, 384, 768), BF16),
            pltpu.VMEM((4, 768, 768), F32),
            dma((4, 2, 2)),
            dma((4,)),
        ),
        [ANY] * 2,
        flops=4 * 10**9,
        size=20 * 2**20,
    )
    (shares,) = call(
        sum_shares_kernel,
        "sum_shares",
        [((16, 48, 896), BF16)],
        [VMEM] * 3,
        (shares.reshape(16, 48, 896), gain_mine, taken_0),
    )
    taken_0, part_out = lax.optimization_barrier((taken_0, part_out))
    out_1 = (middle_1 + summed(with_others(part_out))).astype(BF16)
    grad_proj, grad_out, grad_router, grad_gain_a, grad_gain_m, grad_table = call(
        unpack_kernel,
        "unpack",
        [
            ((3, 192, 768), F32),
            ((192, 768), F32),
            ((32, 768), F32),
            ((1, 768), F32),
            ((1, 768), F32),
            ((3, 32), F32),
        ],
        [VMEM],
        (exchange(shares.reshape(768, 896)),),
    )
    taken_0 = taken_0[:128]
    section_output = jnp.stack(
        [jnp.where(first, low_1, to_second(out_1)), jnp.where(first, taken_1, out_1)]
    )
    input_grad = jnp.stack(
        [
            jnp.where(first, grad_0, taken_1.astype(F32)),
            jnp.where(first, taken_0.astype(F32), grad_1),
        ]
    )
    return (
        section_output[None],
        input_grad[None],
        grad_gain_a,
        grad_proj.transpose(0, 2, 1)[None],
        grad_out[None],
        grad_table[None],
        grad_gain_m,
        grad_router.T[None],
        grad_up[None],
        grad_down[None],
    )


def solution(mesh):
    return jax.shard_map(
        on_device,
        mesh=mesh,
        in_specs=(
            P(None, "expert", None),
            P(None, "expert", None),
            P("section", None, "expert", None),
            P("section", None),
            P("section", None, None, "head"),
            P("section", "head", None),
            P("section", "head", None),
            P("section", None),
            P("section", None, None),
            P("section", "expert", None, "head"),
            P("section", "expert", "head", None),
        ),
        out_specs=(
            P("section", None, "expert", None),
            P("section", None, "expert", None),
            P("section", None),
            P("section", None, None, "head"),
            P("section", "head", None),
            P("section", "head", None),
            P("section", None),
            P("section", None, None),
            P("section", "expert", None, "head"),
            P("section", "expert", "head", None),
        ),
        check_vma=False,
    )
```
